32 devices in a mesh: batch: 4 (over y, core), tensor: 8 (over z, x).
Axes of the slice: x: 2, y: 2, z: 4, core: 2. Of those that a mesh axis runs over, the one named last changes fastest.
Arguments:
- tokens: bfloat16 [16384, 1024], P(('batch', 'tensor')), may hold values from -6 to 6
- gain_attn: float32 [1024], replicated, may hold values from 0.1 to 1.9
- w_qkv: bfloat16 [1024, 1536], P('batch', 'tensor'), may hold values from -0.1875 to 0.1875
- w_attn_out: bfloat16 [1024, 512], P('batch', 'tensor'), may hold values from -0.25 to 0.25
- kv_cache: bfloat16 [512, 128, 1024], P('batch', None, 'tensor'), may hold values from -192 to 192
- page_table: int32 [4, 128], P('batch'), may hold values from 0 to 127, each once within a row
- cached_lengths: int32 [16], P('batch'), may hold values from 1 to 4096, 16384 in all
- gain_moe: float32 [1024], replicated, may hold values from 0.1 to 1.9
- w_router: bfloat16 [1024, 8], replicated, may hold values from -0.1875 to 0.1875
- routes: int32 [16384, 2], P(('batch', 'tensor')), may hold values from 0 to 7, all different within a row; in each aligned block of 512 rows (0 to 511, 512 to 1023, ...) at most 160 rows name the same one
- w_in: bfloat16 [8, 1024, 5632], P('tensor'), may hold values from -0.1875 to 0.1875
- w_out: bfloat16 [8, 2816, 1024], P('tensor'), may hold values from -0.109375 to 0.109375
Outputs:
- mixed: bfloat16 [16384, 1024], P(('batch', 'tensor'))
The draws below stay inside these ranges and needn't reach their ends.
Inputs may be any that keep to these rules, and one draw needn't show every extreme that they name: `page_table`: each row lists all 128 pages of one batch index's pool once; local request r of that batch index reads its cached tokens from entries r * 32 to (r + 1) * 32 - 1 in order. `cached_lengths`: they sum to 16384. `routes`: a token's 2 experts differ; in the rows of one device (512 aligned rows) no expert is named by more than 160 rows, a bound that some block reaches.
All inputs are finite; a program needn't handle non-finite values. No bound on the sum of `cached_lengths` on one device may be relied on, other than what follows from the above.
Results may differ from the reference program's by a relative error of at most 0.012.
Values may be sent and summed in bfloat16 or wider, within the bound.
No kernel may reach another device: no remote copies, remote signals or barrier semaphores. Data moves between devices by JAX's collectives and lax.ppermute only.
A program may use at most 128 MiB of HBM per device.

```python
import math
import jax
import jax.numpy as jnp
import numpy as np
from jax import lax

D = 1024
HD = 64
FF = 2816
TOP = 2
R = 4
SPAN = 1024
PAGE = 128
CACHE_MAX = 4096
CACHE_MEAN = 1024
HEADS = 8
EXPERTS = 8
GROUPS = 4
REQUESTS = 16
TOK_DEV = 512
TOKENS = 16384
MAXPAGES = 32
POOL = 128
CAP = 160


def draw_kv_cache(key, part):
    values = jax.random.normal(jax.random.fold_in(key, 11), (GROUPS * POOL, PAGE, HEADS, 2, HD), jnp.float32)
    values = jnp.clip(values, -4.0, 4.0)
    return values.reshape(GROUPS * POOL, PAGE, HEADS * 2 * HD).astype(jnp.bfloat16)


def block_levels(rng, shape, pieces, smallest, largest):
    level = 1.0
    for axis_at, parts in pieces:
        heights = jax.random.uniform(jax.random.fold_in(jax.random.fold_in(rng, 6), axis_at), (parts,), jnp.float32, smallest / len(pieces), largest / len(pieces))
        level = level * jnp.repeat(jnp.exp(heights), shape[axis_at] // parts).reshape((-1,) + (1,) * (len(shape) - 1 - axis_at))
    return level


def split_up(count, total, limit, slope):
    portions = [(1 << 20) // math.isqrt(rank ** slope) + 1 for rank in range(2, count + 1)]
    rest, counts = total - limit - (count - 1), [1] * (count - 1)
    while rest > 0:
        candidates = [i for i in range(count - 1) if counts[i] < limit]
        whole, left = sum([portions[i] for i in candidates]), rest
        for i in candidates:
            addition = min(limit - counts[i], max(1, left * portions[i] // whole), rest)
            counts[i] = counts[i] + addition
            rest = rest - addition
    return np.array([limit] + counts)


def uneven(key, number_of, total, bound, skew):
    if number_of == 2:
        one = jax.random.randint(key, (), max(1, total - bound), min(bound, total - 1) + 1)
        return jnp.stack([one, total - one])
    sizes = jnp.asarray(split_up(number_of, total, bound, skew), jnp.int32)
    pairs = (number_of - 1) // 2
    donor, receiver = sizes[1:1 + 2 * pairs:2], sizes[2:2 + 2 * pairs:2]
    slack = jnp.minimum(donor - 1, bound - receiver)
    passed = jax.random.randint(jax.random.fold_in(key, 1), (pairs,), 0, 1 << 20) % (slack + 1)
    sizes = sizes.at[1:1 + 2 * pairs:2].set(donor - passed).at[2:2 + 2 * pairs:2].set(receiver + passed)
    return sizes[jax.random.permutation(jax.random.fold_in(key, 2), number_of)]


def deal_out(key, own, number, rows, amount, top, limit, skew):
    sequence = jax.random.permutation(key, amount)
    packed, usual = load_shares(amount, rows * top, limit, skew, True), load_shares(amount, rows * top, limit, skew, False)
    places = jnp.arange(amount)

    def named(lengths, offset_by):
        used = int((lengths > 0).sum())
        fixed = max(1, used // 4)
        passed = fixed + (places - fixed + offset_by * (used - fixed)) % max(1, amount - fixed)
        return jnp.zeros((amount,), jnp.int32).at[sequence[jnp.where(places < fixed, places, passed)]].set(jnp.asarray(lengths, jnp.int32))

    lengths = jnp.where(number % 4 == 0, named(packed, number // 4), named(usual, number - number // 4 - 1))
    mixed = jax.random.permutation(jax.random.fold_in(own, 3), amount)
    donor, receiver = mixed[0:amount // 2 * 2:2], mixed[1:amount // 2 * 2:2]
    room = jnp.minimum(lengths[donor] - 1, limit - lengths[receiver]) // 2
    room = jnp.where((donor == sequence[0]) | (receiver == sequence[0]) | (lengths[receiver] == 0), 0, jnp.maximum(room, 0))
    passed = jax.random.randint(jax.random.fold_in(own, 4), (amount // 2,), 0, 1 << 20) % (room + 1)
    lengths = lengths.at[donor].add(-passed).at[receiver].add(passed)
    members = jnp.searchsorted(jnp.cumsum(lengths), jnp.arange(rows * top), side="right").astype(jnp.int32)
    grid = members.reshape(top, rows).T
    grid = grid[jax.random.permutation(jax.random.fold_in(own, 1), rows)]
    offset_by = jax.random.randint(jax.random.fold_in(own, 2), (rows, 1), 0, top)
    return jnp.take_along_axis(grid, (jnp.arange(top)[None, :] + offset_by) % top, axis=1)


def load_shares(number_of, total, limit, lean, full):
    weights = [(1 << 20) // math.isqrt(standing ** lean) + 1 for standing in range(1, number_of + 1)]
    largest = limit if full else min(limit, max(-(-total // number_of), total * weights[0] // sum(weights)))
    least = 1 if total - largest >= number_of - 1 else 0
    holding, spare = [largest] + [least] * (number_of - 1), total - largest - least * (number_of - 1)
    while spare > 0:
        movable = [i for i in range(1, number_of) if holding[i] < largest] or [i for i in range(1, number_of) if holding[i] < limit]
        pool, budget = sum([weights[i] for i in movable]), spare
        for i in movable:
            extra = min(limit - holding[i], max(1, budget * weights[i] // pool), spare)
            holding[i] = holding[i] + extra
            spare = spare - extra
    return np.array(holding)


def centred(rng, dims, width, limit, shards=(), kind=jnp.bfloat16):
    level = block_levels(rng, dims, shards, -0.22, 0.18) if shards else 1.0
    entries = jax.random.normal(rng, dims, jnp.float32) * width * level
    return jnp.minimum(jnp.maximum(entries, -limit), limit).astype(kind)


def setup_inputs(seed: int = 0) -> dict:
    seeds = jax.random.split(jax.random.key(seed), 13)
    tokens = centred(seeds[0], (TOKENS, D), 1.0, 6.0, ((0, 32),))
    gain_attn = jnp.clip(1.0 + 0.18 * jax.random.normal(seeds[1], (D,), jnp.float32), 0.1, 1.9)
    w_qkv = centred(seeds[2], (D, HEADS * 3 * HD), D ** -0.5, 0.1875, ((0, 4), (1, 8)))
    w_attn_out = centred(seeds[3], (D, HEADS * HD), (HEADS * HD) ** -0.5, 0.25, ((0, 4), (1, 8)))
    kv_cache = draw_kv_cache(jax.random.fold_in(seeds[12], 71), 0)
    page_table = jax.vmap(lambda own: jax.random.permutation(own, POOL))(jax.random.split(seeds[5], GROUPS)).reshape((GROUPS, POOL)).astype(jnp.int32)
    cached_lengths = uneven(seeds[6], REQUESTS, REQUESTS * CACHE_MEAN, CACHE_MAX, 2).astype(jnp.int32)
    gain_moe = jnp.clip(1.0 + 0.18 * jax.random.normal(seeds[7], (D,), jnp.float32), 0.1, 1.9)
    w_router = centred(seeds[8], (D, EXPERTS), D ** -0.5, 0.1875)
    routes_keys = jax.random.split(jax.random.fold_in(seeds[9], 1), TOKENS // TOK_DEV)
    routes_turns = jax.random.permutation(jax.random.fold_in(seeds[9], 3), TOKENS // TOK_DEV)
    routes = jax.vmap(lambda own, number: deal_out(jax.random.fold_in(seeds[9], 2), own, number, TOK_DEV, EXPERTS, TOP, CAP, 2))(routes_keys, routes_turns).reshape((TOKENS, TOP))
    w_in = centred(seeds[10], (EXPERTS, D, 2 * FF), D ** -0.5, 0.1875, ((0, 8),))
    w_out = centred(seeds[11], (EXPERTS, FF, D), FF ** -0.5, 0.109375, ((0, 8),))
    return {"tokens": tokens, "gain_attn": gain_attn, "w_qkv": w_qkv, "w_attn_out": w_attn_out, "kv_cache": kv_cache, "page_table": page_table, "cached_lengths": cached_lengths, "gain_moe": gain_moe, "w_router": w_router, "routes": routes, "w_in": w_in, "w_out": w_out}


EPSILON = 1e-06
NEGATIVE = -1e+30

def rms_norm(values, gain):
    values = values.astype(jnp.float32)
    mean_square = lax.optimization_barrier(jnp.mean(values * values, axis=-1, keepdims=True))
    return values * lax.rsqrt(mean_square + EPSILON) * gain.astype(jnp.float32)

def reference(tokens, gain_attn, w_qkv, w_attn_out, kv_cache, page_table, cached_lengths, gain_moe, w_router, routes, w_in, w_out):
    normed = rms_norm(tokens, gain_attn).astype(jnp.bfloat16)
    projected = jnp.dot(normed, w_qkv, preferred_element_type=jnp.float32).astype(jnp.bfloat16)
    heads_all = w_attn_out.shape[1] // HD
    scale = 1.0 / math.sqrt(HD)
    column = jnp.arange(CACHE_MAX + SPAN, dtype=jnp.int32)
    line = jnp.arange(SPAN, dtype=jnp.int32)

    def one_request(request):
        group = request // R
        local = request % R
        block = lax.dynamic_slice_in_dim(projected, (request * SPAN).astype(jnp.int32), SPAN, 0)
        block = block.reshape(SPAN, heads_all, 3, HD).astype(jnp.float32)
        pages = lax.dynamic_slice_in_dim(page_table[group], (local * MAXPAGES).astype(jnp.int32), MAXPAGES, 0)
        cached = kv_cache[group * POOL + pages].reshape(CACHE_MAX, heads_all, 2, HD).astype(jnp.float32)
        keys = jnp.concatenate([cached[:, :, 0], block[:, :, 1]], axis=0)
        values_all = jnp.concatenate([cached[:, :, 1], block[:, :, 2]], axis=0)
        scores = jnp.einsum('qhd,khd->hqk', block[:, :, 0], keys) * scale
        visible = jnp.where(column[None, :] < CACHE_MAX, column[None, :] < cached_lengths[request], column[None, :] - CACHE_MAX <= line[:, None])
        scores = jnp.where(visible[None], scores, NEGATIVE)
        top_score = lax.optimization_barrier(jnp.max(scores, axis=2, keepdims=True))
        weights = jnp.exp(scores - top_score)
        weights = (weights / lax.optimization_barrier(jnp.sum(weights, axis=2, keepdims=True))).astype(jnp.bfloat16)
        outcome = jnp.einsum('hqk,khd->qhd', weights.astype(jnp.float32), values_all).astype(jnp.bfloat16)
        return outcome.reshape(SPAN, heads_all * HD)
    attended = lax.map(one_request, jnp.arange(REQUESTS, dtype=jnp.int32)).reshape(TOKENS, heads_all * HD)
    projection = jnp.dot(attended, w_attn_out.T, preferred_element_type=jnp.float32)
    state = tokens.astype(jnp.float32) + projection
    normed_moe = rms_norm(state, gain_moe).astype(jnp.bfloat16)
    logits = jnp.dot(normed_moe, w_router, preferred_element_type=jnp.float32)
    picked = jnp.take_along_axis(logits, routes, axis=1)
    squashed = jax.nn.sigmoid(picked)
    gates = squashed / lax.optimization_barrier(jnp.sum(squashed, axis=1, keepdims=True))
    experts = w_router.shape[1]
    blocks = TOKENS // TOK_DEV
    flat_routes = routes.reshape(blocks, TOK_DEV * TOP)
    onehot = (flat_routes[..., None] == jnp.arange(experts, dtype=jnp.int32)).astype(jnp.int32)
    before = jnp.cumsum(onehot, axis=1) - onehot
    slots = lax.optimization_barrier(jnp.sum(before * onehot, axis=-1)).astype(jnp.int32)
    owner_rows = jnp.broadcast_to(jnp.arange(TOK_DEV * TOP, dtype=jnp.int32) // TOP, (blocks, TOK_DEV * TOP))
    flat_gates = gates.reshape(blocks, TOK_DEV * TOP)
    padded = jnp.concatenate([normed_moe.reshape(blocks, TOK_DEV, D), jnp.zeros((blocks, 1, D), jnp.bfloat16)], axis=1)
    block_index = jnp.arange(blocks, dtype=jnp.int32)[:, None]

    def one_expert(total, inputs):
        expert, gate_up, down = inputs
        target = jnp.where(flat_routes == expert, slots, CAP).astype(jnp.int32)
        sources = jnp.full((blocks, CAP), TOK_DEV, jnp.int32).at[block_index, target].set(owner_rows, mode='drop')
        slot_gates = jnp.zeros((blocks, CAP), jnp.float32).at[block_index, target].set(flat_gates, mode='drop')
        gathered = padded[block_index, sources].reshape(blocks * CAP, D)
        inner = jnp.dot(gathered, gate_up, preferred_element_type=jnp.float32)
        active = (jax.nn.gelu(inner[:, :FF], approximate=True) * inner[:, FF:]).astype(jnp.bfloat16)
        outcome = jnp.dot(active, down, preferred_element_type=jnp.float32).astype(jnp.bfloat16).reshape(blocks, CAP, D)
        total = total.at[block_index, sources].add(slot_gates[..., None] * outcome.astype(jnp.float32))
        return (total, None)
    start_total = jnp.zeros((blocks, TOK_DEV + 1, D), jnp.float32)
    total, unused = lax.scan(one_expert, start_total, (jnp.arange(experts, dtype=jnp.int32), w_in, w_out))
    return (state + total[:, :TOK_DEV].reshape(TOKENS, D)).astype(jnp.bfloat16)
```

```python
import functools
import math

import jax
import jax.numpy as jnp
from jax import lax
from jax.experimental import pallas as pl
from jax.experimental.pallas import tpu as pltpu
from jax.sharding import PartitionSpec as P

HD = 64
EXT = 16
EPSILON = 1e-06
NEGATIVE = -1e30
F32, BF16 = jnp.float32, jnp.bfloat16
NT = (((1,), (1,)), ((), ()))
VMEM_LIMIT = 52 * 1024 * 1024
AXES = ("batch", "tensor")


def dot(a, b, dims=(((1,), (0,)), ((), ()))):
    return lax.dot_general(a, b, dims, preferred_element_type=F32)


def vmem(count):
    return [pl.BlockSpec(memory_space=pltpu.VMEM)] * count


def smem(count):
    return [pl.BlockSpec(memory_space=pltpu.SMEM)] * count


def params():
    return pltpu.CompilerParams(vmem_limit_bytes=VMEM_LIMIT)


def send(value, mask, lanes, groups):
    total = lanes * groups
    return lax.ppermute(value, AXES, [(i, i ^ mask) for i in range(total)])


def gather_xor(piece, lanes, groups):
    low = max(1, lanes // 4)
    high = [piece] + [send(piece, s, lanes, groups) for s in range(low, lanes, low)]
    block = jnp.stack(high)
    plane = {}
    for j in range(0, groups, 2):
        for s in range(low):
            mask = j * lanes + s
            plane[(j, s)] = block if mask == 0 else send(block, mask, lanes, groups)
    rows = [jnp.stack([plane[(j, s)] for s in range(low)], axis=1) for j in range(0, groups, 2)]
    half = jnp.stack(rows).reshape((groups // 2, lanes) + piece.shape)
    other = send(half, lanes, lanes, groups)
    return jnp.stack([half, other], axis=1).reshape((groups, lanes) + piece.shape)


def softmax_step(scores, values_ext, m, acc):
    top = jnp.maximum(m, jnp.max(scores, axis=0, keepdims=True))
    weights = jnp.exp(scores - top).astype(BF16)
    return top, acc * jnp.exp(m - top) + dot(values_ext, weights)


def ones_rows(keys):
    return jnp.ones((EXT, keys), BF16)


def cached_kernel(lanes, requests, span_devs, block_pages, *refs):
    info, lengths, table = refs[:3]
    q_refs = refs[3 : 3 + lanes]
    kv_ref = refs[3 + lanes]
    out_refs = refs[4 + lanes : 4 + 2 * lanes]
    q_all, m_ref, acc_ref, out_all = refs[4 + 2 * lanes :]
    page = kv_ref.shape[1]
    pages = table.shape[1] // requests
    rows = q_refs[0].shape[1]
    queries = rows * span_devs
    keys = block_pages * page
    tile = min(256, queries)
    for k in range(requests):
        for i in range(span_devs):
            q_all[k, 0:HD, i * rows : (i + 1) * rows] = q_refs[k * span_devs + i][...]
        q_all[k, HD : 2 * HD, :] = jnp.zeros((HD, queries), BF16)
    first = info[0] // span_devs

    def one_request(k, carry):
        request = jnp.bitwise_xor(first, k)
        length = lengths[request]
        m_ref[...] = jnp.full((1, queries), NEGATIVE, F32)
        acc_ref[...] = jnp.zeros((HD + EXT, queries), F32)

        def block(j, masked):
            parts = [
                kv_ref[
                    table[0, request * pages + jnp.minimum(j * block_pages + n, pages - 1)]
                ]
                for n in range(block_pages)
            ]
            both = jnp.concatenate(parts, axis=0)
            values = jnp.concatenate([both.T[HD : 2 * HD], ones_rows(keys)], axis=0)
            for t in range(0, queries, tile):
                at = pl.ds(t, tile)
                scores = dot(both, q_all[k, :, at])
                if masked:
                    position = j * keys + lax.broadcasted_iota(jnp.int32, scores.shape, 0)
                    scores = jnp.where(position < length, scores, NEGATIVE)
                top, acc = softmax_step(scores, values, m_ref[:, at], acc_ref[:, at])
                m_ref[:, at] = top
                acc_ref[:, at] = acc

        whole = length // keys

        def step(j, c):
            block(j, False)
            return c

        lax.fori_loop(0, whole, step, 0)

        @pl.when(whole * keys < length)
        def _():
            block(whole, True)

        total = acc_ref[HD : HD + 1, :]
        lse = m_ref[...] + jnp.log(total)
        hi = lse.astype(BF16).astype(F32)
        mid = (lse - hi).astype(BF16).astype(F32)
        lo = lse - hi - mid
        at_row = lax.broadcasted_iota(jnp.int32, (EXT, queries), 0)
        stats = jnp.where(
            at_row == 0, hi, jnp.where(at_row == 1, mid, jnp.where(at_row == 2, lo, 0.0))
        )
        out_all[k, 0:HD, :] = (acc_ref[0:HD, :] / total).astype(BF16)
        out_all[k, HD : HD + EXT, :] = stats.astype(BF16)
        return carry

    lax.fori_loop(0, requests, one_request, 0)
    for k in range(requests):
        for i in range(span_devs):
            out_refs[k * span_devs + i][...] = out_all[k, :, i * rows : (i + 1) * rows]


def cached_attention(me, lengths, table, chunks, kv_cache):
    lanes = len(chunks)
    requests = lengths.shape[0]
    span_devs = lanes // requests
    rows = chunks[0].shape[1]
    queries = rows * span_devs
    block_pages = 4
    return pl.pallas_call(
        functools.partial(cached_kernel, lanes, requests, span_devs, block_pages),
        out_shape=[jax.ShapeDtypeStruct((HD + EXT, rows), BF16)] * lanes,
        in_specs=smem(3) + vmem(lanes + 1),
        out_specs=vmem(lanes),
        scratch_shapes=[
            pltpu.VMEM((requests, 2 * HD, queries), BF16),
            pltpu.VMEM((1, queries), F32),
            pltpu.VMEM((HD + EXT, queries), F32),
            pltpu.VMEM((requests, HD + EXT, queries), BF16),
        ],
        compiler_params=params(),
        cost_estimate=pl.CostEstimate(
            flops=8 * 10**9, bytes_accessed=6 * 10**6, transcendentals=8 * 10**6
        ),
        name="cached_attention",
    )(me, lengths, table, *chunks, kv_cache)


def self_kernel(lanes, span_devs, *refs):
    info, q_ref = refs[:2]
    key_refs = refs[2 : 2 + span_devs]
    value_refs = refs[2 + span_devs : 2 + 2 * span_devs]
    out_ref = refs[2 + 2 * span_devs]
    rows = q_ref.shape[1]
    at = info[0] % span_devs

    def pair(j, other, causal):
        block = jnp.bitwise_xor(2 * j, other & ~1) // 2
        keys = key_refs[other][:, pl.ds(pl.multiple_of(block * 2 * HD, 2 * HD), 2 * HD)]
        both_q = q_ref[pl.ds(pl.multiple_of(j * 2 * HD, 2 * HD), 2 * HD), :]
        both_v = value_refs[other][pl.ds(pl.multiple_of(block * 2 * HD, 2 * HD), 2 * HD), :]
        nothing = jnp.zeros((HD, rows), BF16)
        for h in range(2):
            there = h ^ (other & 1)
            q = both_q[h * HD : (h + 1) * HD]
            q = jnp.concatenate([nothing, q] if there else [q, nothing], axis=0)
            scores = dot(keys, q)
            if causal:
                position = lax.broadcasted_iota(jnp.int32, scores.shape, 0)
                line = lax.broadcasted_iota(jnp.int32, scores.shape, 1)
                scores = jnp.where(position <= line, scores, NEGATIVE)
            values = jnp.concatenate([both_v[there * HD : (there + 1) * HD], ones_rows(rows)], axis=0)
            s = 2 * j + h
            if causal:
                m = jnp.full((1, rows), NEGATIVE, F32)
                acc = jnp.zeros((HD + EXT, rows), F32)
            else:
                m = out_ref[s, HD + EXT : HD + EXT + 1, :]
                acc = out_ref[s, 0 : HD + EXT, :]
            top, acc = softmax_step(scores, values, m, acc)
            out_ref[s, 0 : HD + EXT, :] = acc
            out_ref[s, HD + EXT : HD + EXT + 8, :] = jnp.broadcast_to(top, (8, rows))

    def run(other, causal):
        def step(j, c):
            pair(j, other, causal)
            return c

        lax.fori_loop(0, lanes // 2, step, 0)

    run(0, True)
    for other in range(1, span_devs):

        @pl.when(jnp.bitwise_xor(at, other) < at)
        def _(other=other):
            run(other, False)


def self_attention(me, q_t, keys, values):
    span_devs = len(keys)
    lanes = q_t.shape[0] // HD
    rows = q_t.shape[1]
    return pl.pallas_call(
        functools.partial(self_kernel, lanes, span_devs),
        out_shape=jax.ShapeDtypeStruct((lanes, HD + EXT + 8, rows), F32),
        in_specs=smem(1) + vmem(1 + 2 * span_devs),
        out_specs=pl.BlockSpec(memory_space=pltpu.VMEM),
        compiler_params=params(),
        cost_estimate=pl.CostEstimate(
            flops=3 * 10**9, bytes_accessed=5 * 10**6, transcendentals=4 * 10**6
        ),
        name="self_attention",
    )(me, q_t, *keys, *values)


def merge_kernel(lanes, cap, *refs):
    tokens, own = refs[:2]
    cached = refs[2 : 2 + lanes]
    w_o, gain, router, hits, slot_rows = refs[2 + lanes : 7 + lanes]
    state_ref, gates_ref = refs[7 + lanes : 9 + lanes]
    out_refs = refs[9 + lanes : 9 + 2 * lanes]
    attended, placing = refs[9 + 2 * lanes :]
    for s in range(lanes):
        part = cached[s][...].astype(F32)
        lse = part[HD : HD + 1] + part[HD + 1 : HD + 2] + part[HD + 2 : HD + 3]
        m = own[s, HD + EXT : HD + EXT + 1, :]
        total = own[s, HD : HD + 1, :]
        top = jnp.maximum(m, lse)
        w_cached, w_own = jnp.exp(lse - top), jnp.exp(m - top)
        norm = 1.0 / (w_cached + w_own * total)
        merged = part[0:HD] * (w_cached * norm) + own[s, 0:HD, :] * (w_own * norm)
        attended[s * HD : (s + 1) * HD, :] = merged.astype(BF16)
    state = tokens[...].astype(F32) + dot(attended[...].T, w_o[...])
    state_ref[...] = state
    mean_square = jnp.mean(state * state, axis=-1, keepdims=True)
    normed = (state * lax.rsqrt(mean_square + EPSILON) * gain[...]).astype(BF16)
    logits = dot(normed, router[...])
    squashed = jnp.where(hits[...] > 0, jax.nn.sigmoid(logits), 0.0)
    gates_ref[...] = squashed / jnp.sum(squashed, axis=1, keepdims=True)
    rows = tokens.shape[0]
    for s in range(lanes):
        at_slot = lax.broadcasted_iota(jnp.int32, (cap, rows), 0)
        placing[s * cap : (s + 1) * cap, :] = (at_slot == slot_rows[s : s + 1, :]).astype(F32).astype(BF16)
    for s in range(lanes):
        out_refs[s][...] = dot(placing[s * cap : (s + 1) * cap, :], normed).astype(BF16)


def merge_dispatch(tokens, own, cached, w_o, gain, router, hits, slot_rows, cap):
    lanes = len(cached)
    rows, width = tokens.shape
    return pl.pallas_call(
        functools.partial(merge_kernel, lanes, cap),
        out_shape=[
            jax.ShapeDtypeStruct((rows, width), F32),
            jax.ShapeDtypeStruct((rows, lanes), F32),
        ]
        + [jax.ShapeDtypeStruct((cap, width), BF16)] * lanes,
        in_specs=vmem(7 + lanes),
        out_specs=vmem(2 + lanes),
        scratch_shapes=[
            pltpu.VMEM((lanes * HD, rows), BF16),
            pltpu.VMEM((lanes * cap, rows), BF16),
        ],
        compiler_params=params(),
        cost_estimate=pl.CostEstimate(
            flops=4 * 10**9, bytes_accessed=10 * 10**6, transcendentals=10**5
        ),
        name="merge_and_dispatch",
    )(tokens, own, *cached, w_o, gain, router, hits, slot_rows)


def expert_kernel(count, *refs):
    x_refs = refs[:count]
    gate_ref, up_ref, down_ref = refs[count : count + 3]
    out_refs = refs[count + 3 : 2 * count + 3]
    x_all, total = refs[2 * count + 3 :]
    cap = x_refs[0].shape[0]
    step = pl.program_id(0)

    @pl.when(step == 0)
    def _():
        for n in range(count):
            x_all[n * cap : (n + 1) * cap, :] = x_refs[n][...]

    x = x_all[...]
    gate = dot(x, gate_ref[0])
    up = dot(x, up_ref[0])
    active = (jax.nn.gelu(gate, approximate=True) * up).astype(BF16)
    part = dot(active, down_ref[0])

    @pl.when(step == 0)
    def _():
        total[...] = part

    @pl.when(step > 0)
    def _():
        total[...] += part

    @pl.when(step == pl.num_programs(0) - 1)
    def _():
        for n in range(count):
            out_refs[n][...] = total[n * cap : (n + 1) * cap, :].astype(BF16)


def expert(chunks, w_in, w_out):
    count = len(chunks)
    cap, width = chunks[0].shape
    hidden = w_out.shape[1]
    tile = 256
    steps = hidden // tile
    whole = pl.BlockSpec((cap, width), lambda j: (0, 0))
    return pl.pallas_call(
        functools.partial(expert_kernel, count),
        grid=(steps,),
        out_shape=[jax.ShapeDtypeStruct((cap, width), BF16)] * count,
        in_specs=[whole] * count
        + [
            pl.BlockSpec((1, width, tile), lambda j: (0, 0, j)),
            pl.BlockSpec((1, width, tile), lambda j: (0, 0, j + steps)),
            pl.BlockSpec((1, tile, width), lambda j: (0, j, 0)),
        ],
        out_specs=[whole] * count,
        scratch_shapes=[
            pltpu.VMEM((count * cap, width), BF16),
            pltpu.VMEM((count * cap, width), F32),
        ],
        compiler_params=params(),
        cost_estimate=pl.CostEstimate(
            flops=6 * count * cap * width * hidden,
            bytes_accessed=6 * width * hidden,
            transcendentals=count * cap * hidden,
        ),
        name="expert",
    )(*chunks, w_in, w_in, w_out)


def combine_kernel(first, count, last, *refs):
    base, gates, slots = refs[:3]
    parts = refs[3 : 3 + count]
    out = refs[3 + count]
    rows = base.shape[0]
    cap = parts[0].shape[0]
    total = base[...]
    for n in range(count):
        s = first + n
        lane = lax.broadcasted_iota(jnp.int32, (rows, cap), 1)
        pick = (lane == slots[:, s : s + 1]).astype(F32).astype(BF16)
        total = total + gates[:, s : s + 1] * dot(pick, parts[n][...])
    out[...] = total.astype(out.dtype)


def combine(base, gates, slots, parts, first, last):
    count = len(parts)
    rows, width = base.shape
    return pl.pallas_call(
        functools.partial(combine_kernel, first, count, last),
        out_shape=jax.ShapeDtypeStruct((rows, width), BF16 if last else F32),
        in_specs=vmem(3 + count),
        out_specs=pl.BlockSpec(memory_space=pltpu.VMEM),
        compiler_params=params(),
        cost_estimate=pl.CostEstimate(
            flops=2 * count * rows * parts[0].shape[0] * width,
            bytes_accessed=6 * 10**6,
            transcendentals=0,
        ),
        name="combine",
    )(base, gates, slots, *parts)


def body(
    tokens,
    gain_attn,
    w_qkv,
    w_attn_out,
    kv_cache,
    page_table,
    cached_lengths,
    gain_moe,
    w_router,
    routes,
    w_in,
    w_out,
):
    lanes, groups = lax.axis_size("tensor"), lax.axis_size("batch")
    me, group = lax.axis_index("tensor"), lax.axis_index("batch")
    rows, width = tokens.shape
    requests = cached_lengths.shape[0]
    span_devs = lanes // requests
    share = width // groups
    here = me.astype(jnp.int32).reshape(1)

    w_t = w_qkv.T
    w_q = gather_xor(w_t[0:HD] * (1.0 / math.sqrt(HD)), lanes, groups)
    rest = jnp.concatenate([w_t[HD : 3 * HD], w_attn_out.T], axis=0)
    rest, w_q = lax.optimization_barrier((rest, w_q))
    w_rest = gather_xor(rest, lanes, groups)

    values = tokens.astype(F32)
    mean_square = jnp.mean(values * values, axis=-1, keepdims=True)
    normed = (values * lax.rsqrt(mean_square + EPSILON) * gain_attn).astype(BF16)
    normed = jnp.concatenate(
        [lax.dynamic_slice_in_dim(normed, (group ^ j) * share, share, 1) for j in range(groups)],
        axis=1,
    )

    def columns(pieces):
        return pieces.transpose(1, 2, 0, 3).reshape(lanes * HD, groups * share)

    q_t = dot(columns(w_q), normed, NT).astype(BF16)
    q_chunks = [q_t[s * HD : (s + 1) * HD] for s in range(lanes)]
    order = sorted(range(1, lanes), key=lambda s: -s)
    q_in = {0: q_chunks[0]}
    for s in order:
        q_in[s] = send(q_chunks[s], s, lanes, groups)

    keys = dot(normed, columns(w_rest[:, :, 0:HD]), NT).astype(BF16)
    vals = dot(columns(w_rest[:, :, HD : 2 * HD]), normed, NT).astype(BF16)
    near_keys, near_vals = [keys], [vals]
    for i in range(1, span_devs):
        pairs = [
            (b * lanes + t, b * lanes + (t ^ i))
            for b in range(groups)
            for t in range(lanes)
            if t % span_devs < (t ^ i) % span_devs
        ]
        near_keys.append(lax.ppermute(keys, AXES, pairs))
        near_vals.append(lax.ppermute(vals, AXES, pairs))
    o_pieces = w_rest[:, :, 2 * HD : 3 * HD].reshape(groups, lanes * HD, share)
    w_o = jnp.concatenate(
        [lax.dynamic_index_in_dim(o_pieces, group ^ n, 0, keepdims=False) for n in range(groups)],
        axis=1,
    )

    parts = cached_attention(
        here, cached_lengths, page_table, [q_in[s] for s in range(lanes)], kv_cache
    )
    back = {0: parts[0]}
    for s in order:
        back[s] = send(parts[s], s, lanes, groups)
    own = self_attention(here, q_t, near_keys, near_vals)

    names = me ^ jnp.arange(lanes, dtype=jnp.int32)
    hit_rows = (routes[:, 0][None, :] == names[:, None]) | (routes[:, 1][None, :] == names[:, None])
    earlier = jnp.triu(jnp.ones((rows, rows), BF16), 1)
    rank = dot(hit_rows.astype(BF16), earlier).astype(jnp.int32)
    slot_rows = jnp.where(hit_rows, rank, -1)
    slots = slot_rows.T
    hits = hit_rows.astype(jnp.int32).T
    capacity = max(2, (5 * rows * routes.shape[1] + 4 * lanes - 1) // (4 * lanes))
    cap = -(-capacity // 16) * 16
    router = jnp.take(w_router, names, axis=1)

    outcome = merge_dispatch(
        tokens,
        own,
        [back[s] for s in range(lanes)],
        w_o,
        gain_moe.reshape(1, width),
        router,
        hits,
        slot_rows,
        cap,
    )
    state, gates, buffers = outcome[0], outcome[1], outcome[2:]
    arrived = {0: buffers[0]}
    for s in order:
        arrived[s] = send(buffers[s], s, lanes, groups)
    half = lanes // 2
    mixed = state
    for first in (0, half):
        mine = range(first, first + half)
        results = expert([arrived[s] for s in mine], w_in, w_out)
        returned = [
            results[n] if s == 0 else send(results[n], s, lanes, groups)
            for n, s in enumerate(mine)
        ]
        mixed = combine(mixed, gates, slots, returned, first, first == half)
    return mixed


def solution(mesh):
    in_specs = (
        P(("batch", "tensor"), None),
        P(),
        P("batch", "tensor"),
        P("batch", "tensor"),
        P("batch", None, "tensor"),
        P("batch", None),
        P("batch"),
        P(),
        P(),
        P(("batch", "tensor"), None),
        P("tensor", None, None),
        P("tensor", None, None),
    )
    out_specs = P(("batch", "tensor"), None)
    return jax.shard_map(body, mesh=mesh, in_specs=in_specs, out_specs=out_specs, check_vma=False)
```

```python
import functools
import math

import jax
import jax.numpy as jnp
from jax import lax
from jax.experimental import pallas as pl
from jax.experimental.pallas import tpu as pltpu
from jax.sharding import PartitionSpec as P

HD = 64
EXT = 16
EPSILON = 1e-06
NEGATIVE = -1e30
F32, BF16 = jnp.float32, jnp.bfloat16
NT = (((1,), (1,)), ((), ()))
VMEM_LIMIT = 52 * 1024 * 1024
AXES = ("batch", "tensor")


def dot(a, b, dims=(((1,), (0,)), ((), ()))):
    return lax.dot_general(a, b, dims, preferred_element_type=F32)


def vmem(count):
    return [pl.BlockSpec(memory_space=pltpu.VMEM)] * count


def smem(count):
    return [pl.BlockSpec(memory_space=pltpu.SMEM)] * count


def params():
    return pltpu.CompilerParams(vmem_limit_bytes=VMEM_LIMIT)


def send(value, mask, lanes, groups):
    total = lanes * groups
    return lax.ppermute(value, AXES, [(i, i ^ mask) for i in range(total)])


def gather_high(piece, lanes, groups):
    low = max(1, lanes // 4)
    return jnp.stack([piece] + [send(piece, s, lanes, groups) for s in range(low, lanes, low)])


def gather_plane(block, lanes, groups):
    low = max(1, lanes // 4)
    rows = []
    for j in range(0, groups, 2):
        masks = [j * lanes + s for s in range(low)]
        rows.append(
            jnp.stack([send(block, m, lanes, groups) if m else block for m in masks], axis=1)
        )
    return jnp.stack(rows).reshape((groups // 2, lanes) + block.shape[1:])


def after(value, *others):
    return lax.optimization_barrier((value,) + others)[0]


def ones_rows(keys):
    return jnp.ones((EXT, keys), BF16)


def softmax_steps(scores, values, old):
    tops = [jnp.maximum(m, jnp.max(s, axis=0, keepdims=True)) for s, (m, acc) in zip(scores, old)]
    return [
        (top, acc * jnp.exp2(m - top) + dot(v, jnp.exp2(s - top).astype(BF16)))
        for s, v, top, (m, acc) in zip(scores, values, tops, old)
    ]


def cached_kernel(requests, span_devs, block_pages, lengths, table, q_ref, kv_ref, out_ref, q_all, m_ref, acc_ref):
    page = kv_ref.shape[1]
    pages = table.shape[1] // requests
    rows = q_ref.shape[2]
    queries = rows * span_devs
    keys = block_pages * page
    tile = min(256, queries)
    tiles = [slice(t, t + tile) for t in range(0, queries, tile)]
    q_all[HD : 2 * HD, :] = jnp.zeros((HD, queries), BF16)

    def one_request(request, carry):
        length = lengths[request]
        for i in range(span_devs):
            q_all[0:HD, i * rows : (i + 1) * rows] = q_ref[request * span_devs + i]
        m_ref[...] = jnp.full((1, queries), NEGATIVE, F32)
        acc_ref[...] = jnp.zeros((HD + EXT, queries), F32)

        def block(j, masked):
            parts = [
                kv_ref[
                    table[0, request * pages + jnp.minimum(j * block_pages + n, pages - 1)]
                ]
                for n in range(block_pages)
            ]
            both = jnp.concatenate(parts, axis=0)
            values = jnp.concatenate([both.T[HD : 2 * HD], ones_rows(keys)], axis=0)
            scores = [dot(both, q_all[:, at]) for at in tiles]
            if masked:
                position = j * keys + lax.broadcasted_iota(jnp.int32, scores[0].shape, 0)
                scores = [jnp.where(position < length, s, NEGATIVE) for s in scores]
            old = [(m_ref[:, at], acc_ref[:, at]) for at in tiles]
            new = softmax_steps(scores, [values] * len(tiles), old)
            for at, (top, acc) in zip(tiles, new):
                m_ref[:, at] = top
                acc_ref[:, at] = acc

        whole = length // keys

        def step(j, c):
            block(j, False)
            return c

        lax.fori_loop(0, whole, step, 0)

        @pl.when(whole * keys < length)
        def _():
            block(whole, True)

        total = acc_ref[HD : HD + 1, :]
        lse = m_ref[...] + jnp.log2(total)
        hi = lse.astype(BF16).astype(F32)
        mid = (lse - hi).astype(BF16).astype(F32)
        lo = lse - hi - mid
        at_row = lax.broadcasted_iota(jnp.int32, (EXT, queries), 0)
        stats = jnp.where(
            at_row == 0, hi, jnp.where(at_row == 1, mid, jnp.where(at_row == 2, lo, 0.0))
        ).astype(BF16)
        values = (acc_ref[0:HD, :] * (1.0 / total)).astype(BF16)
        for i in range(span_devs):
            at = slice(i * rows, (i + 1) * rows)
            out_ref[request * span_devs + i, 0:HD, :] = values[:, at]
            out_ref[request * span_devs + i, HD : HD + EXT, :] = stats[:, at]
        return carry

    lax.fori_loop(0, requests, one_request, 0)


def cached_attention(lengths, table, q, kv_cache):
    lanes, _, rows = q.shape
    requests = lengths.shape[0]
    span_devs = lanes // requests
    queries = rows * span_devs
    return pl.pallas_call(
        functools.partial(cached_kernel, requests, span_devs, 4),
        out_shape=jax.ShapeDtypeStruct((lanes, HD + EXT, rows), BF16),
        in_specs=smem(2) + vmem(2),
        out_specs=pl.BlockSpec(memory_space=pltpu.VMEM),
        scratch_shapes=[
            pltpu.VMEM((2 * HD, queries), BF16),
            pltpu.VMEM((1, queries), F32),
            pltpu.VMEM((HD + EXT, queries), F32),
        ],
        compiler_params=params(),
        cost_estimate=pl.CostEstimate(
            flops=8 * 10**9, bytes_accessed=6 * 10**6, transcendentals=8 * 10**6
        ),
        name="cached_attention",
    )(lengths, table, q, kv_cache)


def query_kernel(scale, info, normed, even, odd, out_ref):
    lanes, _, rows = out_ref.shape
    halves, _, _, share = even.shape
    total = jnp.zeros((lanes * HD, rows), F32)
    for n in range(halves):
        for low, ref in enumerate((even, odd)):
            at = jnp.bitwise_xor(info[1], 2 * n + low) * share
            columns = normed[:, pl.ds(pl.multiple_of(at, share), share)]
            total = total + dot(ref[n].reshape(lanes * HD, share), columns, NT)
    q = (total * scale).astype(BF16)
    for s in range(lanes):
        out_ref[jnp.bitwise_xor(info[0], s)] = q[s * HD : (s + 1) * HD]


def project_queries(info, normed, even, odd):
    lanes = even.shape[1]
    rows = normed.shape[0]
    scale = math.log2(math.e) / math.sqrt(HD)
    return pl.pallas_call(
        functools.partial(query_kernel, scale),
        out_shape=jax.ShapeDtypeStruct((lanes, HD, rows), BF16),
        in_specs=smem(1) + vmem(3),
        out_specs=pl.BlockSpec(memory_space=pltpu.VMEM),
        compiler_params=params(),
        cost_estimate=pl.CostEstimate(flops=10**9, bytes_accessed=2 * 10**6, transcendentals=0),
        name="project_queries",
    )(info, normed, even, odd)


def self_kernel(span_devs, *refs):
    info, q_ref = refs[:2]
    normed_refs = refs[2 : 2 + span_devs]
    even, odd = refs[2 + span_devs : 4 + span_devs]
    out_ref, w_o_ref, w_k, w_v, keys_ref, values_ref = refs[5 + span_devs :]
    lanes, _, rows = q_ref.shape
    halves, _, _, share = even.shape
    groups = 2 * halves
    me, group = info[0], info[1]
    at = me % span_devs

    for n in range(halves):
        for low, ref in enumerate((even, odd)):
            column = pl.ds(
                pl.multiple_of(jnp.bitwise_xor(group, 2 * n + low) * share, share), share
            )
            for h in range(lanes):
                piece = ref[n, jnp.bitwise_xor(me, h)]
                head = slice(h * HD, (h + 1) * HD)
                w_k[head, column] = piece[0:HD]
                w_v[head, column] = piece[HD : 2 * HD]
                w_o_ref[head, column] = piece[2 * HD : 3 * HD]

    def project(normed):
        keys_ref[...] = dot(normed[...], w_k[...], NT).astype(BF16)
        values_ref[...] = dot(w_v[...], normed[...], NT).astype(BF16)

    together = 4
    tile = min(256, rows)

    def run(causal):
        def step(g, carry):
            scores, values, old, places = [], [], [], []
            nothing = jnp.zeros((HD, tile), BF16)
            for p in range(together // 2):
                block = pl.multiple_of((g * together + 2 * p) * HD, 2 * HD)
                keys = keys_ref[:, pl.ds(block, 2 * HD)]
                both_v = values_ref[pl.ds(block, 2 * HD), :]
                for h in range(2):
                    s = g * together + 2 * p + h
                    q = q_ref[s]
                    value = jnp.concatenate([both_v[h * HD : (h + 1) * HD], ones_rows(rows)], axis=0)
                    for t in range(0, rows, tile):
                        here = slice(t, t + tile)
                        seen = t + tile if causal else rows
                        part = [nothing, q[:, here]] if h else [q[:, here], nothing]
                        score = dot(keys[0:seen], jnp.concatenate(part, axis=0))
                        if causal:
                            position = lax.broadcasted_iota(jnp.int32, score.shape, 0)
                            line = t + lax.broadcasted_iota(jnp.int32, score.shape, 1)
                            score = jnp.where(position <= line, score, NEGATIVE)
                            m = jnp.full((1, tile), NEGATIVE, F32)
                            acc = jnp.zeros((HD + EXT, tile), F32)
                        else:
                            m = out_ref[s, HD + EXT : HD + EXT + 1, here]
                            acc = out_ref[s, 0 : HD + EXT, here]
                        scores.append(score)
                        values.append(value[:, 0:seen])
                        old.append((m, acc))
                        places.append((s, here))
            for (s, here), (top, acc) in zip(places, softmax_steps(scores, values, old)):
                out_ref[s, 0 : HD + EXT, here] = acc
                out_ref[s, HD + EXT : HD + EXT + 8, here] = jnp.broadcast_to(top, (8, tile))
            return carry

        lax.fori_loop(0, lanes // together, step, 0)

    project(normed_refs[0])
    run(True)
    for other in range(1, span_devs):

        @pl.when(jnp.bitwise_xor(at, other) < at)
        def _(other=other):
            project(normed_refs[other])
            run(False)


def self_attention(info, q, normed, even, odd, earlier):
    span_devs = len(normed)
    lanes, _, rows = q.shape
    width = normed[0].shape[1]
    anywhere = [pl.BlockSpec(memory_space=pl.ANY)]
    return pl.pallas_call(
        functools.partial(self_kernel, span_devs),
        out_shape=[
            jax.ShapeDtypeStruct((lanes, HD + EXT + 8, rows), F32),
            jax.ShapeDtypeStruct((lanes * HD, width), BF16),
        ],
        in_specs=smem(1) + vmem(3 + span_devs) + anywhere,
        out_specs=vmem(2),
        scratch_shapes=[
            pltpu.VMEM((lanes * HD, width), BF16),
            pltpu.VMEM((lanes * HD, width), BF16),
            pltpu.VMEM((rows, lanes * HD), BF16),
            pltpu.VMEM((lanes * HD, rows), BF16),
        ],
        compiler_params=params(),
        cost_estimate=pl.CostEstimate(
            flops=4 * 10**9, bytes_accessed=5 * 10**6, transcendentals=4 * 10**6
        ),
        name="self_attention",
    )(info, q, *normed, even, odd, earlier)


def fill(out_refs, which, normed, slot_rows, placing):
    cap = out_refs[0].shape[0]
    rows = normed.shape[0]
    for n, s in enumerate(which):
        at_slot = lax.broadcasted_iota(jnp.int32, (cap, rows), 0)
        placing[n * cap : (n + 1) * cap, :] = (
            (at_slot == slot_rows[s : s + 1, :]).astype(F32).astype(BF16)
        )
    for n in range(len(which)):
        out_refs[n][...] = dot(placing[n * cap : (n + 1) * cap, :], normed).astype(BF16)


def dispatch_kernel(which, *refs):
    normed, slot_rows = refs[:2]
    out_refs = refs[3 : 3 + len(which)]
    fill(out_refs, which, normed[...], slot_rows, refs[3 + len(which)])


def dispatch(normed, slot_rows, which, cap, earlier):
    rows, width = normed.shape
    return pl.pallas_call(
        functools.partial(dispatch_kernel, tuple(which)),
        out_shape=[jax.ShapeDtypeStruct((cap, width), BF16)] * len(which),
        in_specs=vmem(2) + [pl.BlockSpec(memory_space=pl.ANY)],
        out_specs=vmem(len(which)),
        scratch_shapes=[pltpu.VMEM((len(which) * cap, rows), BF16)],
        compiler_params=params(),
        cost_estimate=pl.CostEstimate(
            flops=2 * len(which) * cap * rows * width, bytes_accessed=10**6, transcendentals=0
        ),
        name="dispatch",
    )(normed, slot_rows, earlier)


def merge_kernel(which, tokens, own, cached, w_o, gain, router, hits, slot_rows, *refs):
    state_ref, gates_ref, normed_ref = refs[:3]
    out_refs = refs[3 : 3 + len(which)]
    attended, placing = refs[3 + len(which) :]
    for s in range(own.shape[0]):
        part = cached[s].astype(F32)
        lse = part[HD : HD + 1] + part[HD + 1 : HD + 2] + part[HD + 2 : HD + 3]
        m = own[s, HD + EXT : HD + EXT + 1, :]
        total = own[s, HD : HD + 1, :]
        top = jnp.maximum(m, lse)
        w_cached, w_own = jnp.exp2(lse - top), jnp.exp2(m - top)
        norm = 1.0 / (w_cached + w_own * total)
        merged = part[0:HD] * (w_cached * norm) + own[s, 0:HD, :] * (w_own * norm)
        attended[s * HD : (s + 1) * HD, :] = merged.astype(BF16)
    state = tokens[...].astype(F32) + dot(attended[...].T, w_o[...])
    state_ref[...] = state
    mean_square = jnp.mean(state * state, axis=-1, keepdims=True)
    normed = (state * lax.rsqrt(mean_square + EPSILON) * gain[...]).astype(BF16)
    logits = dot(normed, router[...])
    squashed = jnp.where(hits[...] > 0, jax.nn.sigmoid(logits), 0.0)
    gates_ref[...] = squashed / jnp.sum(squashed, axis=1, keepdims=True)
    normed_ref[...] = normed
    fill(out_refs, which, normed, slot_rows, placing)


def merge_dispatch(tokens, own, cached, w_o, gain, router, hits, slot_rows, which, cap):
    lanes = own.shape[0]
    rows, width = tokens.shape
    return pl.pallas_call(
        functools.partial(merge_kernel, tuple(which)),
        out_shape=[
            jax.ShapeDtypeStruct((rows, width), F32),
            jax.ShapeDtypeStruct((rows, lanes), F32),
            jax.ShapeDtypeStruct((rows, width), BF16),
        ]
        + [jax.ShapeDtypeStruct((cap, width), BF16)] * len(which),
        in_specs=vmem(8),
        out_specs=vmem(3 + len(which)),
        scratch_shapes=[
            pltpu.VMEM((lanes * HD, rows), BF16),
            pltpu.VMEM((len(which) * cap, rows), BF16),
        ],
        compiler_params=params(),
        cost_estimate=pl.CostEstimate(
            flops=4 * 10**9, bytes_accessed=10 * 10**6, transcendentals=10**5
        ),
        name="merge_and_dispatch",
    )(tokens, own, cached, w_o, gain, router, hits, slot_rows)


def expert_kernel(count, *refs):
    x_refs = refs[:count]
    gate_ref, up_ref, down_ref = refs[count : count + 3]
    out_refs = refs[count + 4 : 2 * count + 4]
    x_all, total = refs[2 * count + 4 :]
    cap = x_refs[0].shape[0]
    step = pl.program_id(0)

    @pl.when(step == 0)
    def _():
        for n in range(count):
            x_all[n * cap : (n + 1) * cap, :] = x_refs[n][...]

    x = x_all[...]
    gate = dot(x, gate_ref[0])
    up = dot(x, up_ref[0])
    active = (jax.nn.gelu(gate, approximate=True) * up).astype(BF16)
    part = dot(active, down_ref[0])

    @pl.when(step == 0)
    def _():
        total[...] = part

    @pl.when(step > 0)
    def _():
        total[...] += part

    @pl.when(step == pl.num_programs(0) - 1)
    def _():
        for n in range(count):
            out_refs[n][...] = total[n * cap : (n + 1) * cap, :].astype(BF16)


def expert(chunks, w_in, w_out, earlier):
    count = len(chunks)
    cap, width = chunks[0].shape
    hidden = w_out.shape[1]
    tile = 256
    steps = hidden // tile
    whole = pl.BlockSpec((cap, width), lambda j: (0, 0))
    return pl.pallas_call(
        functools.partial(expert_kernel, count),
        grid=(steps,),
        out_shape=[jax.ShapeDtypeStruct((cap, width), BF16)] * count,
        in_specs=[whole] * count
        + [
            pl.BlockSpec((1, width, tile), lambda j: (0, 0, j)),
            pl.BlockSpec((1, width, tile), lambda j: (0, 0, j + steps)),
            pl.BlockSpec((1, tile, width), lambda j: (0, j, 0)),
            pl.BlockSpec(memory_space=pl.ANY),
        ],
        out_specs=[whole] * count,
        scratch_shapes=[
            pltpu.VMEM((count * cap, width), BF16),
            pltpu.VMEM((count * cap, width), F32),
        ],
        compiler_params=params(),
        cost_estimate=pl.CostEstimate(
            flops=6 * count * cap * width * hidden,
            bytes_accessed=6 * width * hidden,
            transcendentals=count * cap * hidden,
        ),
        name="expert",
    )(*chunks, w_in, w_in, w_out, earlier)


def combine_kernel(first, count, last, *refs):
    base, gates, slots = refs[:3]
    parts = refs[3 : 3 + count]
    out = refs[3 + count]
    rows = base.shape[0]
    cap = parts[0].shape[0]
    total = base[...]
    for n in range(count):
        s = first + n
        lane = lax.broadcasted_iota(jnp.int32, (rows, cap), 1)
        pick = (lane == slots[:, s : s + 1]).astype(F32).astype(BF16)
        total = total + gates[:, s : s + 1] * dot(pick, parts[n][...])
    out[...] = total.astype(out.dtype)


def combine(base, gates, slots, parts, first, last):
    count = len(parts)
    rows, width = base.shape
    return pl.pallas_call(
        functools.partial(combine_kernel, first, count, last),
        out_shape=jax.ShapeDtypeStruct((rows, width), BF16 if last else F32),
        in_specs=vmem(3 + count),
        out_specs=pl.BlockSpec(memory_space=pltpu.VMEM),
        compiler_params=params(),
        cost_estimate=pl.CostEstimate(
            flops=2 * count * rows * parts[0].shape[0] * width,
            bytes_accessed=6 * 10**6,
            transcendentals=0,
        ),
        name="combine",
    )(base, gates, slots, *parts)


def body(
    tokens,
    gain_attn,
    w_qkv,
    w_attn_out,
    kv_cache,
    page_table,
    cached_lengths,
    gain_moe,
    w_router,
    routes,
    w_in,
    w_out,
):
    lanes, groups = lax.axis_size("tensor"), lax.axis_size("batch")
    me, group = lax.axis_index("tensor"), lax.axis_index("batch")
    rows, width = tokens.shape
    requests = cached_lengths.shape[0]
    span_devs = lanes // requests
    share = width // groups
    info = jnp.stack([me, group]).astype(jnp.int32)

    w_t = w_qkv.T
    q_plane = gather_plane(gather_high(w_t[0:HD], lanes, groups), lanes, groups)
    q_other = send(q_plane, lanes, lanes, groups)
    values = tokens.astype(F32)
    mean_square = jnp.mean(values * values, axis=-1, keepdims=True)
    normed = (values * lax.rsqrt(mean_square + EPSILON) * gain_attn).astype(BF16)
    q = project_queries(info, normed, q_plane, q_other)
    q_here = lax.all_to_all(q, "tensor", split_axis=0, concat_axis=0, tiled=True)

    near = [normed]
    ready = after(normed, q_plane)
    for i in range(1, span_devs):
        pairs = [
            (b * lanes + t, b * lanes + (t ^ i))
            for b in range(groups)
            for t in range(lanes)
            if t % span_devs < (t ^ i) % span_devs
        ]
        near.append(lax.ppermute(ready, AXES, pairs))
    rest = jnp.concatenate([w_t[HD : 3 * HD], w_attn_out.T], axis=0)
    rest = gather_high(after(rest, q_other), lanes, groups)
    rest = gather_plane(rest, lanes, groups)
    rest_other = send(rest, lanes, lanes, groups)

    parts = cached_attention(cached_lengths, page_table, q_here, kv_cache)
    cached = lax.all_to_all(parts, "tensor", split_axis=0, concat_axis=0, tiled=True)
    own, w_o = self_attention(info, q, near, rest, rest_other, parts)

    names = me ^ jnp.arange(lanes, dtype=jnp.int32)
    hit_rows = (routes[:, 0][None, :] == names[:, None]) | (routes[:, 1][None, :] == names[:, None])
    earlier = jnp.triu(jnp.ones((rows, rows), BF16), 1)
    rank = dot(hit_rows.astype(BF16), earlier).astype(jnp.int32)
    slot_rows = jnp.where(hit_rows, rank, -1)
    slots = slot_rows.T
    hits = hit_rows.astype(jnp.int32).T
    capacity = max(2, (5 * rows * routes.shape[1] + 4 * lanes - 1) // (4 * lanes))
    cap = -(-capacity // 16) * 16
    router = jnp.take(w_router, names, axis=1)

    half, quarter = lanes // 2, lanes // 4
    near = list(range(half))
    far = [list(range(half, half + quarter)), list(range(half + quarter, lanes))]
    outcome = merge_dispatch(
        tokens,
        own,
        cached,
        w_o,
        gain_moe.reshape(1, width),
        router,
        hits,
        slot_rows,
        far[0] + near,
        cap,
    )
    state, gates, normed_moe = outcome[:3]
    buffers = dict(zip(far[0] + near, outcome[3:]))
    arrived = {s: send(buffers[s], s, lanes, groups) if s else buffers[s] for s in buffers}
    buffers.update(zip(far[1], dispatch(normed_moe, slot_rows, far[1], cap, arrived[near[-1]])))
    arrived.update({s: send(buffers[s], s, lanes, groups) for s in far[1]})
    mixed = state
    results = [gates]
    for part in (near, far[0], far[1]):
        results = expert([arrived[s] for s in part], w_in, w_out, results[0])
        returned = [
            results[n] if s == 0 else send(results[n], s, lanes, groups)
            for n, s in enumerate(part)
        ]
        mixed = combine(mixed, gates, slots, returned, part[0], part is far[1])
    return mixed


def solution(mesh):
    in_specs = (
        P(("batch", "tensor"), None),
        P(),
        P("batch", "tensor"),
        P("batch", "tensor"),
        P("batch", None, "tensor"),
        P("batch", None),
        P("batch"),
        P(),
        P(),
        P(("batch", "tensor"), None),
        P("tensor", None, None),
        P("tensor", None, None),
    )
    out_specs = P(("batch", "tensor"), None)
    return jax.shard_map(body, mesh=mesh, in_specs=in_specs, out_specs=out_specs, check_vma=False)
```

```python
import functools
import math

import jax
import jax.numpy as jnp
from jax import lax
from jax.experimental import pallas as pl
from jax.experimental.pallas import tpu as pltpu
from jax.sharding import PartitionSpec as P

HD = 64
EXT = 16
EPSILON = 1e-06
NEGATIVE = -1e30
F32, BF16 = jnp.float32, jnp.bfloat16
NT = (((1,), (1,)), ((), ()))
VMEM_LIMIT = 52 * 1024 * 1024
AXES = ("batch", "tensor")


def dot(a, b, dims=(((1,), (0,)), ((), ()))):
    return lax.dot_general(a, b, dims, preferred_element_type=F32)


def vmem(count):
    return [pl.BlockSpec(memory_space=pltpu.VMEM)] * count


def smem(count):
    return [pl.BlockSpec(memory_space=pltpu.SMEM)] * count


def params():
    return pltpu.CompilerParams(vmem_limit_bytes=VMEM_LIMIT)


def send(value, mask, lanes, groups):
    total = lanes * groups
    return lax.ppermute(value, AXES, [(i, i ^ mask) for i in range(total)])


def gather_high(piece, lanes, groups):
    low = max(1, lanes // 4)
    return jnp.stack([piece] + [send(piece, s, lanes, groups) for s in range(low, lanes, low)])


def gather_plane(block, lanes, groups):
    low = max(1, lanes // 4)
    rows = []
    for j in range(0, groups, 2):
        masks = [j * lanes + s for s in range(low)]
        rows.append(
            jnp.stack([send(block, m, lanes, groups) if m else block for m in masks], axis=1)
        )
    return jnp.stack(rows).reshape((groups // 2, lanes) + block.shape[1:])


def after(value, *others):
    return lax.optimization_barrier((value,) + others)[0]


def ones_rows(keys):
    return jnp.ones((EXT, keys), BF16)


def softmax_steps(scores, values, old):
    tops = [jnp.maximum(m, jnp.max(s, axis=0, keepdims=True)) for s, (m, acc) in zip(scores, old)]
    return [
        (top, acc * jnp.exp2(m - top) + dot(v, jnp.exp2(s - top).astype(BF16)))
        for s, v, top, (m, acc) in zip(scores, values, tops, old)
    ]


def cached_kernel(requests, span_devs, block_pages, lengths, table, q_ref, kv_ref, out_ref, q_all, m_ref, acc_ref):
    page = kv_ref.shape[1]
    pages = table.shape[1] // requests
    rows = q_ref.shape[2]
    queries = rows * span_devs
    keys = block_pages * page
    tile = min(256, queries)
    tiles = [slice(t, t + tile) for t in range(0, queries, tile)]
    q_all[HD : 2 * HD, :] = jnp.zeros((HD, queries), BF16)

    def one_request(request, carry):
        length = lengths[request]
        for i in range(span_devs):
            q_all[0:HD, i * rows : (i + 1) * rows] = q_ref[request * span_devs + i]
        m_ref[...] = jnp.full((1, queries), NEGATIVE, F32)
        acc_ref[...] = jnp.zeros((HD + EXT, queries), F32)

        def block(j, masked):
            parts = [
                kv_ref[
                    table[0, request * pages + jnp.minimum(j * block_pages + n, pages - 1)]
                ]
                for n in range(block_pages)
            ]
            both = jnp.concatenate(parts, axis=0)
            values = jnp.concatenate([both.T[HD : 2 * HD], ones_rows(keys)], axis=0)
            scores = [dot(both, q_all[:, at]) for at in tiles]
            if masked:
                position = j * keys + lax.broadcasted_iota(jnp.int32, scores[0].shape, 0)
                scores = [jnp.where(position < length, s, NEGATIVE) for s in scores]
            old = [(m_ref[:, at], acc_ref[:, at]) for at in tiles]
            new = softmax_steps(scores, [values] * len(tiles), old)
            for at, (top, acc) in zip(tiles, new):
                m_ref[:, at] = top
                acc_ref[:, at] = acc

        whole = length // keys

        def step(j, c):
            block(j, False)
            return c

        lax.fori_loop(0, whole, step, 0)

        @pl.when(whole * keys < length)
        def _():
            block(whole, True)

        total = acc_ref[HD : HD + 1, :]
        lse = m_ref[...] + jnp.log2(total)
        hi = lse.astype(BF16).astype(F32)
        mid = (lse - hi).astype(BF16).astype(F32)
        lo = lse - hi - mid
        at_row = lax.broadcasted_iota(jnp.int32, (EXT, queries), 0)
        stats = jnp.where(
            at_row == 0, hi, jnp.where(at_row == 1, mid, jnp.where(at_row == 2, lo, 0.0))
        ).astype(BF16)
        values = (acc_ref[0:HD, :] * (1.0 / total)).astype(BF16)
        for i in range(span_devs):
            at = slice(i * rows, (i + 1) * rows)
            out_ref[request * span_devs + i, 0:HD, :] = values[:, at]
            out_ref[request * span_devs + i, HD : HD + EXT, :] = stats[:, at]
        return carry

    lax.fori_loop(0, requests, one_request, 0)


def cached_attention(lengths, table, q, kv_cache):
    lanes, _, rows = q.shape
    requests = lengths.shape[0]
    span_devs = lanes // requests
    queries = rows * span_devs
    return pl.pallas_call(
        functools.partial(cached_kernel, requests, span_devs, 4),
        out_shape=jax.ShapeDtypeStruct((lanes, HD + EXT, rows), BF16),
        in_specs=smem(2) + vmem(2),
        out_specs=pl.BlockSpec(memory_space=pltpu.VMEM),
        scratch_shapes=[
            pltpu.VMEM((2 * HD, queries), BF16),
            pltpu.VMEM((1, queries), F32),
            pltpu.VMEM((HD + EXT, queries), F32),
        ],
        compiler_params=params(),
        cost_estimate=pl.CostEstimate(
            flops=8 * 10**9, bytes_accessed=6 * 10**6, transcendentals=8 * 10**6
        ),
        name="cached_attention",
    )(lengths, table, q, kv_cache)


def query_kernel(scale, info, normed, even, odd, out_ref):
    lanes, _, rows = out_ref.shape
    halves, _, _, share = even.shape
    total = jnp.zeros((lanes * HD, rows), F32)
    for n in range(halves):
        for low, ref in enumerate((even, odd)):
            at = jnp.bitwise_xor(info[1], 2 * n + low) * share
            columns = normed[:, pl.ds(pl.multiple_of(at, share), share)]
            total = total + dot(ref[n].reshape(lanes * HD, share), columns, NT)
    q = (total * scale).astype(BF16)
    for s in range(lanes):
        out_ref[jnp.bitwise_xor(info[0], s)] = q[s * HD : (s + 1) * HD]


def project_queries(info, normed, even, odd):
    lanes = even.shape[1]
    rows = normed.shape[0]
    scale = math.log2(math.e) / math.sqrt(HD)
    return pl.pallas_call(
        functools.partial(query_kernel, scale),
        out_shape=jax.ShapeDtypeStruct((lanes, HD, rows), BF16),
        in_specs=smem(1) + vmem(3),
        out_specs=pl.BlockSpec(memory_space=pltpu.VMEM),
        compiler_params=params(),
        cost_estimate=pl.CostEstimate(flops=10**9, bytes_accessed=2 * 10**6, transcendentals=0),
        name="project_queries",
    )(info, normed, even, odd)


def self_kernel(span_devs, *refs):
    info, q_ref = refs[:2]
    normed_refs = refs[2 : 2 + span_devs]
    even, odd = refs[2 + span_devs : 4 + span_devs]
    out_ref, w_o_ref, w_k, w_v, keys_ref, values_ref = refs[5 + span_devs :]
    lanes, _, rows = q_ref.shape
    halves, _, _, share = even.shape
    groups = 2 * halves
    me, group = info[0], info[1]
    at = me % span_devs

    for n in range(halves):
        for low, ref in enumerate((even, odd)):
            column = pl.ds(
                pl.multiple_of(jnp.bitwise_xor(group, 2 * n + low) * share, share), share
            )
            for h in range(lanes):
                piece = ref[n, jnp.bitwise_xor(me, h)]
                head = slice(h * HD, (h + 1) * HD)
                w_k[head, column] = piece[0:HD]
                w_v[head, column] = piece[HD : 2 * HD]
                w_o_ref[head, column] = piece[2 * HD : 3 * HD]

    def project(normed):
        keys_ref[...] = dot(normed[...], w_k[...], NT).astype(BF16)
        values_ref[...] = dot(w_v[...], normed[...], NT).astype(BF16)

    together = 4
    tile = min(256, rows)

    def run(causal):
        def step(g, carry):
            scores, values, old, places = [], [], [], []
            nothing = jnp.zeros((HD, tile), BF16)
            for p in range(together // 2):
                block = pl.multiple_of((g * together + 2 * p) * HD, 2 * HD)
                keys = keys_ref[:, pl.ds(block, 2 * HD)]
                both_v = values_ref[pl.ds(block, 2 * HD), :]
                for h in range(2):
                    s = g * together + 2 * p + h
                    q = q_ref[s]
                    value = jnp.concatenate([both_v[h * HD : (h + 1) * HD], ones_rows(rows)], axis=0)
                    for t in range(0, rows, tile):
                        here = slice(t, t + tile)
                        seen = t + tile if causal else rows
                        part = [nothing, q[:, here]] if h else [q[:, here], nothing]
                        score = dot(keys[0:seen], jnp.concatenate(part, axis=0))
                        if causal:
                            position = lax.broadcasted_iota(jnp.int32, score.shape, 0)
                            line = t + lax.broadcasted_iota(jnp.int32, score.shape, 1)
                            score = jnp.where(position <= line, score, NEGATIVE)
                            m = jnp.full((1, tile), NEGATIVE, F32)
                            acc = jnp.zeros((HD + EXT, tile), F32)
                        else:
                            m = out_ref[s, HD + EXT : HD + EXT + 1, here]
                            acc = out_ref[s, 0 : HD + EXT, here]
                        scores.append(score)
                        values.append(value[:, 0:seen])
                        old.append((m, acc))
                        places.append((s, here))
            for (s, here), (top, acc) in zip(places, softmax_steps(scores, values, old)):
                out_ref[s, 0 : HD + EXT, here] = acc
                out_ref[s, HD + EXT : HD + EXT + 8, here] = jnp.broadcast_to(top, (8, tile))
            return carry

        lax.fori_loop(0, lanes // together, step, 0)

    project(normed_refs[0])
    run(True)
    for other in range(1, span_devs):

        @pl.when(jnp.bitwise_xor(at, other) < at)
        def _(other=other):
            project(normed_refs[other])
            run(False)


def self_attention(info, q, normed, even, odd, earlier):
    span_devs = len(normed)
    lanes, _, rows = q.shape
    width = normed[0].shape[1]
    anywhere = [pl.BlockSpec(memory_space=pl.ANY)]
    return pl.pallas_call(
        functools.partial(self_kernel, span_devs),
        out_shape=[
            jax.ShapeDtypeStruct((lanes, HD + EXT + 8, rows), F32),
            jax.ShapeDtypeStruct((lanes * HD, width), BF16),
        ],
        in_specs=smem(1) + vmem(3 + span_devs) + anywhere,
        out_specs=vmem(2),
        scratch_shapes=[
            pltpu.VMEM((lanes * HD, width), BF16),
            pltpu.VMEM((lanes * HD, width), BF16),
            pltpu.VMEM((rows, lanes * HD), BF16),
            pltpu.VMEM((lanes * HD, rows), BF16),
        ],
        compiler_params=params(),
        cost_estimate=pl.CostEstimate(
            flops=4 * 10**9, bytes_accessed=5 * 10**6, transcendentals=4 * 10**6
        ),
        name="self_attention",
    )(info, q, *normed, even, odd, earlier)


def fill(out_refs, which, normed, slot_rows, placing):
    cap = out_refs[0].shape[0]
    rows = normed.shape[0]
    for n, s in enumerate(which):
        at_slot = lax.broadcasted_iota(jnp.int32, (cap, rows), 0)
        placing[n * cap : (n + 1) * cap, :] = (
            (at_slot == slot_rows[s : s + 1, :]).astype(F32).astype(BF16)
        )
    for n in range(len(which)):
        out_refs[n][...] = dot(placing[n * cap : (n + 1) * cap, :], normed).astype(BF16)


def dispatch_kernel(which, *refs):
    normed, slot_rows = refs[:2]
    out_refs = refs[3 : 3 + len(which)]
    fill(out_refs, which, normed[...], slot_rows, refs[3 + len(which)])


def dispatch(normed, slot_rows, which, cap, earlier):
    rows, width = normed.shape
    return pl.pallas_call(
        functools.partial(dispatch_kernel, tuple(which)),
        out_shape=[jax.ShapeDtypeStruct((cap, width), BF16)] * len(which),
        in_specs=vmem(2) + [pl.BlockSpec(memory_space=pl.ANY)],
        out_specs=vmem(len(which)),
        scratch_shapes=[pltpu.VMEM((len(which) * cap, rows), BF16)],
        compiler_params=params(),
        cost_estimate=pl.CostEstimate(
            flops=2 * len(which) * cap * rows * width, bytes_accessed=10**6, transcendentals=0
        ),
        name="dispatch",
    )(normed, slot_rows, earlier)


def merge_kernel(which, tokens, own, cached, w_o, gain, router, hits, slot_rows, *refs):
    state_ref, gates_ref, normed_ref = refs[:3]
    out_refs = refs[3 : 3 + len(which)]
    attended, placing = refs[3 + len(which) :]
    for s in range(own.shape[0]):
        part = cached[s].astype(F32)
        lse = part[HD : HD + 1] + part[HD + 1 : HD + 2] + part[HD + 2 : HD + 3]
        m = own[s, HD + EXT : HD + EXT + 1, :]
        total = own[s, HD : HD + 1, :]
        top = jnp.maximum(m, lse)
        w_cached, w_own = jnp.exp2(lse - top), jnp.exp2(m - top)
        norm = 1.0 / (w_cached + w_own * total)
        merged = part[0:HD] * (w_cached * norm) + own[s, 0:HD, :] * (w_own * norm)
        attended[s * HD : (s + 1) * HD, :] = merged.astype(BF16)
    state = tokens[...].astype(F32) + dot(attended[...].T, w_o[...])
    state_ref[...] = state
    mean_square = jnp.mean(state * state, axis=-1, keepdims=True)
    normed = (state * lax.rsqrt(mean_square + EPSILON) * gain[...]).astype(BF16)
    logits = dot(normed, router[...])
    squashed = jnp.where(hits[...] > 0, jax.nn.sigmoid(logits), 0.0)
    gates_ref[...] = squashed / jnp.sum(squashed, axis=1, keepdims=True)
    normed_ref[...] = normed
    fill(out_refs, which, normed, slot_rows, placing)


def merge_dispatch(tokens, own, cached, w_o, gain, router, hits, slot_rows, which, cap):
    lanes = own.shape[0]
    rows, width = tokens.shape
    return pl.pallas_call(
        functools.partial(merge_kernel, tuple(which)),
        out_shape=[
            jax.ShapeDtypeStruct((rows, width), F32),
            jax.ShapeDtypeStruct((rows, lanes), F32),
            jax.ShapeDtypeStruct((rows, width), BF16),
        ]
        + [jax.ShapeDtypeStruct((cap, width), BF16)] * len(which),
        in_specs=vmem(8),
        out_specs=vmem(3 + len(which)),
        scratch_shapes=[
            pltpu.VMEM((lanes * HD, rows), BF16),
            pltpu.VMEM((len(which) * cap, rows), BF16),
        ],
        compiler_params=params(),
        cost_estimate=pl.CostEstimate(
            flops=4 * 10**9, bytes_accessed=10 * 10**6, transcendentals=10**5
        ),
        name="merge_and_dispatch",
    )(tokens, own, cached, w_o, gain, router, hits, slot_rows)


def expert_kernel(count, *refs):
    x_refs = refs[:count]
    gate_ref, up_ref, down_ref = refs[count : count + 3]
    out_refs = refs[count + 4 : 2 * count + 4]
    x_all, total = refs[2 * count + 4 :]
    cap = x_refs[0].shape[0]
    step = pl.program_id(0)

    @pl.when(step == 0)
    def _():
        for n in range(count):
            x_all[n * cap : (n + 1) * cap, :] = x_refs[n][...]

    x = x_all[...]
    gate = dot(x, gate_ref[0])
    up = dot(x, up_ref[0])
    active = (jax.nn.gelu(gate, approximate=True) * up).astype(BF16)
    part = dot(active, down_ref[0])

    @pl.when(step == 0)
    def _():
        total[...] = part

    @pl.when(step > 0)
    def _():
        total[...] += part

    @pl.when(step == pl.num_programs(0) - 1)
    def _():
        for n in range(count):
            out_refs[n][...] = total[n * cap : (n + 1) * cap, :].astype(BF16)


def expert(chunks, w_in, w_out, earlier):
    count = len(chunks)
    cap, width = chunks[0].shape
    hidden = w_out.shape[1]
    tile = 256
    steps = hidden // tile
    whole = pl.BlockSpec((cap, width), lambda j: (0, 0))
    return pl.pallas_call(
        functools.partial(expert_kernel, count),
        grid=(steps,),
        out_shape=[jax.ShapeDtypeStruct((cap, width), BF16)] * count,
        in_specs=[whole] * count
        + [
            pl.BlockSpec((1, width, tile), lambda j: (0, 0, j)),
            pl.BlockSpec((1, width, tile), lambda j: (0, 0, j + steps)),
            pl.BlockSpec((1, tile, width), lambda j: (0, j, 0)),
            pl.BlockSpec(memory_space=pl.ANY),
        ],
        out_specs=[whole] * count,
        scratch_shapes=[
            pltpu.VMEM((count * cap, width), BF16),
            pltpu.VMEM((count * cap, width), F32),
        ],
        compiler_params=params(),
        cost_estimate=pl.CostEstimate(
            flops=6 * count * cap * width * hidden,
            bytes_accessed=6 * width * hidden,
            transcendentals=count * cap * hidden,
        ),
        name="expert",
    )(*chunks, w_in, w_in, w_out, earlier)


def combine_kernel(first, count, last, *refs):
    base, gates, slots = refs[:3]
    parts = refs[3 : 3 + count]
    out = refs[3 + count]
    rows = base.shape[0]
    cap = parts[0].shape[0]
    total = base[...]
    for n in range(count):
        s = first + n
        lane = lax.broadcasted_iota(jnp.int32, (rows, cap), 1)
        pick = (lane == slots[:, s : s + 1]).astype(F32).astype(BF16)
        total = total + gates[:, s : s + 1] * dot(pick, parts[n][...])
    out[...] = total.astype(out.dtype)


def combine(base, gates, slots, parts, first, last):
    count = len(parts)
    rows, width = base.shape
    return pl.pallas_call(
        functools.partial(combine_kernel, first, count, last),
        out_shape=jax.ShapeDtypeStruct((rows, width), BF16 if last else F32),
        in_specs=vmem(3 + count),
        out_specs=pl.BlockSpec(memory_space=pltpu.VMEM),
        compiler_params=params(),
        cost_estimate=pl.CostEstimate(
            flops=2 * count * rows * parts[0].shape[0] * width,
            bytes_accessed=6 * 10**6,
            transcendentals=0,
        ),
        name="combine",
    )(base, gates, slots, *parts)


def body(
    tokens,
    gain_attn,
    w_qkv,
    w_attn_out,
    kv_cache,
    page_table,
    cached_lengths,
    gain_moe,
    w_router,
    routes,
    w_in,
    w_out,
):
    lanes, groups = lax.axis_size("tensor"), lax.axis_size("batch")
    me, group = lax.axis_index("tensor"), lax.axis_index("batch")
    rows, width = tokens.shape
    requests = cached_lengths.shape[0]
    span_devs = lanes // requests
    share = width // groups
    info = jnp.stack([me, group]).astype(jnp.int32)

    w_t = w_qkv.T
    q_high = gather_high(w_t[0:HD], lanes, groups)
    q_plane = gather_plane(q_high, lanes, groups)
    q_other = send(q_plane, lanes, lanes, groups)
    values = tokens.astype(F32)
    mean_square = jnp.mean(values * values, axis=-1, keepdims=True)
    normed = (values * lax.rsqrt(mean_square + EPSILON) * gain_attn).astype(BF16)
    q = project_queries(info, normed, q_plane, q_other)
    q_here = lax.all_to_all(q, "tensor", split_axis=0, concat_axis=0, tiled=True)

    near = [normed]
    rest = jnp.concatenate([w_t[HD : 3 * HD], w_attn_out.T], axis=0)
    ready, rest = lax.optimization_barrier((normed, rest, q))[:2]
    for i in range(1, span_devs):
        pairs = [
            (b * lanes + t, b * lanes + (t ^ i))
            for b in range(groups)
            for t in range(lanes)
            if t % span_devs < (t ^ i) % span_devs
        ]
        near.append(lax.ppermute(ready, AXES, pairs))
    rest = gather_high(rest, lanes, groups)
    rest = gather_plane(after(rest, *near[1:]), lanes, groups)

    parts = cached_attention(cached_lengths, page_table, q_here, kv_cache)
    rest_other = send(after(rest, parts), lanes, lanes, groups)
    cached = lax.all_to_all(parts, "tensor", split_axis=0, concat_axis=0, tiled=True)
    own, w_o = self_attention(info, q, near, rest, rest_other, parts)

    names = me ^ jnp.arange(lanes, dtype=jnp.int32)
    hit_rows = (routes[:, 0][None, :] == names[:, None]) | (routes[:, 1][None, :] == names[:, None])
    earlier = jnp.triu(jnp.ones((rows, rows), BF16), 1)
    rank = dot(hit_rows.astype(BF16), earlier).astype(jnp.int32)
    slot_rows = jnp.where(hit_rows, rank, -1)
    slots = slot_rows.T
    hits = hit_rows.astype(jnp.int32).T
    capacity = max(2, (5 * rows * routes.shape[1] + 4 * lanes - 1) // (4 * lanes))
    cap = -(-capacity // 16) * 16
    router = jnp.take(w_router, names, axis=1)

    half, quarter = lanes // 2, lanes // 4
    near = list(range(half))
    far = [list(range(half, half + quarter)), list(range(half + quarter, lanes))]
    outcome = merge_dispatch(
        tokens,
        own,
        cached,
        w_o,
        gain_moe.reshape(1, width),
        router,
        hits,
        slot_rows,
        far[0] + near,
        cap,
    )
    state, gates, normed_moe = outcome[:3]
    buffers = dict(zip(far[0] + near, outcome[3:]))
    arrived = {s: send(buffers[s], s, lanes, groups) if s else buffers[s] for s in buffers}
    buffers.update(zip(far[1], dispatch(normed_moe, slot_rows, far[1], cap, arrived[near[-1]])))
    arrived.update({s: send(buffers[s], s, lanes, groups) for s in far[1]})
    mixed = state
    results = [gates]
    for part in (near, far[0], far[1]):
        results = expert([arrived[s] for s in part], w_in, w_out, results[0])
        returned = [
            results[n] if s == 0 else send(results[n], s, lanes, groups)
            for n, s in enumerate(part)
        ]
        mixed = combine(mixed, gates, slots, returned, part[0], part is far[1])
    return mixed


def solution(mesh):
    in_specs = (
        P(("batch", "tensor"), None),
        P(),
        P("batch", "tensor"),
        P("batch", "tensor"),
        P("batch", None, "tensor"),
        P("batch", None),
        P("batch"),
        P(),
        P(),
        P(("batch", "tensor"), None),
        P("tensor", None, None),
        P("tensor", None, None),
    )
    out_specs = P(("batch", "tensor"), None)
    return jax.shard_map(body, mesh=mesh, in_specs=in_specs, out_specs=out_specs, check_vma=False)
```

```python
import functools
import math

import jax
import jax.numpy as jnp
from jax import lax
from jax.experimental import pallas as pl
from jax.experimental.pallas import tpu as pltpu
from jax.sharding import PartitionSpec as P

HD = 64
EXT = 16
EPSILON = 1e-06
NEGATIVE = -1e30
F32, BF16 = jnp.float32, jnp.bfloat16
NT = (((1,), (1,)), ((), ()))
VMEM_LIMIT = 52 * 1024 * 1024
AXES = ("batch", "tensor")


def dot(a, b, dims=(((1,), (0,)), ((), ()))):
    return lax.dot_general(a, b, dims, preferred_element_type=F32)


def rms_norm(values, gain):
    values = values.astype(F32)
    mean_square = jnp.mean(values * values, axis=-1, keepdims=True)
    return (values * lax.rsqrt(mean_square + EPSILON) * gain).astype(BF16)


def vmem(count):
    return [pl.BlockSpec(memory_space=pltpu.VMEM)] * count


def smem(count):
    return [pl.BlockSpec(memory_space=pltpu.SMEM)] * count


def params():
    return pltpu.CompilerParams(vmem_limit_bytes=VMEM_LIMIT)


def send(value, mask, lanes, groups):
    total = lanes * groups
    return lax.ppermute(value, AXES, [(i, i ^ mask) for i in range(total)])


def gather_high(piece, lanes, groups):
    low = max(1, lanes // 4)
    return jnp.stack([piece] + [send(piece, s, lanes, groups) for s in range(low, lanes, low)])


def gather_plane(block, lanes, groups):
    low = max(1, lanes // 4)
    rows = []
    for j in range(0, groups, 2):
        masks = [j * lanes + s for s in range(low)]
        rows.append(
            jnp.stack([send(block, m, lanes, groups) if m else block for m in masks], axis=1)
        )
    return jnp.stack(rows).reshape((groups // 2, lanes) + block.shape[1:])


def after(value, *others):
    return lax.optimization_barrier((value,) + others)[0]


def ones_rows(keys):
    return jnp.ones((EXT, keys), BF16)


def softmax_steps(scores, values, old):
    tops = [jnp.maximum(m, jnp.max(s, axis=0, keepdims=True)) for s, (m, acc) in zip(scores, old)]
    return [
        (top, acc * jnp.exp2(m - top) + dot(v, jnp.exp2(s - top).astype(BF16)))
        for s, v, top, (m, acc) in zip(scores, values, tops, old)
    ]


def cached_kernel(requests, span_devs, block_pages, lengths, table, q_ref, kv_ref, out_ref, q_all, m_ref, acc_ref):
    page = kv_ref.shape[1]
    pages = table.shape[1] // requests
    rows = q_ref.shape[2]
    queries = rows * span_devs
    keys = block_pages * page
    tile = min(256, queries)
    tiles = [slice(t, t + tile) for t in range(0, queries, tile)]
    q_all[HD : 2 * HD, :] = jnp.zeros((HD, queries), BF16)

    def one_request(request, carry):
        length = lengths[request]
        for i in range(span_devs):
            q_all[0:HD, i * rows : (i + 1) * rows] = q_ref[request * span_devs + i]
        m_ref[...] = jnp.full((1, queries), NEGATIVE, F32)
        acc_ref[...] = jnp.zeros((HD + EXT, queries), F32)

        def block(j, masked):
            parts = [
                kv_ref[
                    table[0, request * pages + jnp.minimum(j * block_pages + n, pages - 1)]
                ]
                for n in range(block_pages)
            ]
            both = jnp.concatenate(parts, axis=0)
            values = jnp.concatenate([both.T[HD : 2 * HD], ones_rows(keys)], axis=0)
            scores = [dot(both, q_all[:, at]) for at in tiles]
            if masked:
                position = j * keys + lax.broadcasted_iota(jnp.int32, scores[0].shape, 0)
                scores = [jnp.where(position < length, s, NEGATIVE) for s in scores]
            old = [(m_ref[:, at], acc_ref[:, at]) for at in tiles]
            new = softmax_steps(scores, [values] * len(tiles), old)
            for at, (top, acc) in zip(tiles, new):
                m_ref[:, at] = top
                acc_ref[:, at] = acc

        whole = length // keys

        def step(j, c):
            block(j, False)
            return c

        lax.fori_loop(0, whole, step, 0)

        @pl.when(whole * keys < length)
        def _():
            block(whole, True)

        total = acc_ref[HD : HD + 1, :]
        lse = m_ref[...] + jnp.log2(total)
        hi = lse.astype(BF16).astype(F32)
        mid = (lse - hi).astype(BF16).astype(F32)
        lo = lse - hi - mid
        at_row = lax.broadcasted_iota(jnp.int32, (EXT, queries), 0)
        stats = jnp.where(
            at_row == 0, hi, jnp.where(at_row == 1, mid, jnp.where(at_row == 2, lo, 0.0))
        ).astype(BF16)
        values = (acc_ref[0:HD, :] * (1.0 / total)).astype(BF16)
        for i in range(span_devs):
            at = slice(i * rows, (i + 1) * rows)
            out_ref[request * span_devs + i, 0:HD, :] = values[:, at]
            out_ref[request * span_devs + i, HD : HD + EXT, :] = stats[:, at]
        return carry

    lax.fori_loop(0, requests, one_request, 0)


def cached_attention(lengths, table, q, kv_cache):
    lanes, _, rows = q.shape
    requests = lengths.shape[0]
    span_devs = lanes // requests
    queries = rows * span_devs
    return pl.pallas_call(
        functools.partial(cached_kernel, requests, span_devs, 4),
        out_shape=jax.ShapeDtypeStruct((lanes, HD + EXT, rows), BF16),
        in_specs=smem(2) + vmem(2),
        out_specs=pl.BlockSpec(memory_space=pltpu.VMEM),
        scratch_shapes=[
            pltpu.VMEM((2 * HD, queries), BF16),
            pltpu.VMEM((1, queries), F32),
            pltpu.VMEM((HD + EXT, queries), F32),
        ],
        compiler_params=params(),
        cost_estimate=pl.CostEstimate(
            flops=8 * 10**9, bytes_accessed=6 * 10**6, transcendentals=8 * 10**6
        ),
        name="cached_attention",
    )(lengths, table, q, kv_cache)


def query_kernel(scale, info, normed, even, odd, out_ref):
    lanes, _, rows = out_ref.shape
    halves, _, _, share = even.shape
    total = jnp.zeros((lanes * HD, rows), F32)
    for n in range(halves):
        for low, ref in enumerate((even, odd)):
            at = jnp.bitwise_xor(info[1], 2 * n + low) * share
            columns = normed[:, pl.ds(pl.multiple_of(at, share), share)]
            total = total + dot(ref[n].reshape(lanes * HD, share), columns, NT)
    q = (total * scale).astype(BF16)
    for s in range(lanes):
        out_ref[jnp.bitwise_xor(info[0], s)] = q[s * HD : (s + 1) * HD]


def project_queries(info, normed, even, odd):
    lanes = even.shape[1]
    rows = normed.shape[0]
    scale = math.log2(math.e) / math.sqrt(HD)
    return pl.pallas_call(
        functools.partial(query_kernel, scale),
        out_shape=jax.ShapeDtypeStruct((lanes, HD, rows), BF16),
        in_specs=smem(1) + vmem(3),
        out_specs=pl.BlockSpec(memory_space=pltpu.VMEM),
        compiler_params=params(),
        cost_estimate=pl.CostEstimate(flops=10**9, bytes_accessed=2 * 10**6, transcendentals=0),
        name="project_queries",
    )(info, normed, even, odd)


def self_kernel(span_devs, *refs):
    info, q_ref = refs[:2]
    normed_refs = refs[2 : 2 + span_devs]
    even, odd = refs[2 + span_devs : 4 + span_devs]
    out_ref, w_o_ref, w_k, w_v, keys_ref, values_ref = refs[5 + span_devs :]
    lanes, _, rows = q_ref.shape
    halves, _, _, share = even.shape
    groups = 2 * halves
    me, group = info[0], info[1]
    at = me % span_devs

    for n in range(halves):
        for low, ref in enumerate((even, odd)):
            column = pl.ds(
                pl.multiple_of(jnp.bitwise_xor(group, 2 * n + low) * share, share), share
            )
            for h in range(lanes):
                piece = ref[n, jnp.bitwise_xor(me, h)]
                head = slice(h * HD, (h + 1) * HD)
                w_k[head, column] = piece[0:HD]
                w_v[head, column] = piece[HD : 2 * HD]
                w_o_ref[head, column] = piece[2 * HD : 3 * HD]

    def project(normed):
        keys_ref[...] = dot(normed[...], w_k[...], NT).astype(BF16)
        values_ref[...] = dot(w_v[...], normed[...], NT).astype(BF16)

    together = 4
    tile = min(256, rows)

    def run(causal):
        def step(g, carry):
            scores, values, old, places = [], [], [], []
            nothing = jnp.zeros((HD, tile), BF16)
            for p in range(together // 2):
                block = pl.multiple_of((g * together + 2 * p) * HD, 2 * HD)
                keys = keys_ref[:, pl.ds(block, 2 * HD)]
                both_v = values_ref[pl.ds(block, 2 * HD), :]
                for h in range(2):
                    s = g * together + 2 * p + h
                    q = q_ref[s]
                    value = jnp.concatenate([both_v[h * HD : (h + 1) * HD], ones_rows(rows)], axis=0)
                    for t in range(0, rows, tile):
                        here = slice(t, t + tile)
                        seen = t + tile if causal else rows
                        part = [nothing, q[:, here]] if h else [q[:, here], nothing]
                        score = dot(keys[0:seen], jnp.concatenate(part, axis=0))
                        if causal:
                            position = lax.broadcasted_iota(jnp.int32, score.shape, 0)
                            line = t + lax.broadcasted_iota(jnp.int32, score.shape, 1)
                            score = jnp.where(position <= line, score, NEGATIVE)
                            m = jnp.full((1, tile), NEGATIVE, F32)
                            acc = jnp.zeros((HD + EXT, tile), F32)
                        else:
                            m = out_ref[s, HD + EXT : HD + EXT + 1, here]
                            acc = out_ref[s, 0 : HD + EXT, here]
                        scores.append(score)
                        values.append(value[:, 0:seen])
                        old.append((m, acc))
                        places.append((s, here))
            for (s, here), (top, acc) in zip(places, softmax_steps(scores, values, old)):
                out_ref[s, 0 : HD + EXT, here] = acc
                out_ref[s, HD + EXT : HD + EXT + 8, here] = jnp.broadcast_to(top, (8, tile))
            return carry

        lax.fori_loop(0, lanes // together, step, 0)

    project(normed_refs[0])
    run(True)
    for other in range(1, span_devs):

        @pl.when(jnp.bitwise_xor(at, other) < at)
        def _(other=other):
            project(normed_refs[other])
            run(False)


def self_attention(info, q, normed, even, odd, earlier):
    span_devs = len(normed)
    lanes, _, rows = q.shape
    width = normed[0].shape[1]
    anywhere = [pl.BlockSpec(memory_space=pl.ANY)]
    return pl.pallas_call(
        functools.partial(self_kernel, span_devs),
        out_shape=[
            jax.ShapeDtypeStruct((lanes, HD + EXT + 8, rows), F32),
            jax.ShapeDtypeStruct((lanes * HD, width), BF16),
        ],
        in_specs=smem(1) + vmem(3 + span_devs) + anywhere,
        out_specs=vmem(2),
        scratch_shapes=[
            pltpu.VMEM((lanes * HD, width), BF16),
            pltpu.VMEM((lanes * HD, width), BF16),
            pltpu.VMEM((rows, lanes * HD), BF16),
            pltpu.VMEM((lanes * HD, rows), BF16),
        ],
        compiler_params=params(),
        cost_estimate=pl.CostEstimate(
            flops=4 * 10**9, bytes_accessed=5 * 10**6, transcendentals=4 * 10**6
        ),
        name="self_attention",
    )(info, q, *normed, even, odd, earlier)


def fill(out_refs, which, values, slot_rows, placing):
    cap = out_refs[0].shape[0]
    rows = values.shape[0]
    for n, s in enumerate(which):
        at_slot = lax.broadcasted_iota(jnp.int32, (cap, rows), 0)
        placing[n * cap : (n + 1) * cap, :] = (
            (at_slot == slot_rows[s : s + 1, :]).astype(F32).astype(BF16)
        )
    rows_out = dot(placing[0 : len(which) * cap, :], values).astype(BF16)
    for n in range(len(which)):
        out_refs[n][...] = rows_out[n * cap : (n + 1) * cap, :]


def dispatch_kernel(which, *refs):
    normed, slot_rows = refs[:2]
    out_refs = refs[3 : 3 + len(which)]
    fill(out_refs, which, normed[...], slot_rows, refs[3 + len(which)])


def dispatch(normed, slot_rows, which, cap, earlier):
    rows, width = normed.shape
    return pl.pallas_call(
        functools.partial(dispatch_kernel, tuple(which)),
        out_shape=[jax.ShapeDtypeStruct((cap, width), BF16)] * len(which),
        in_specs=vmem(2) + [pl.BlockSpec(memory_space=pl.ANY)],
        out_specs=vmem(len(which)),
        scratch_shapes=[pltpu.VMEM((len(which) * cap, rows), BF16)],
        compiler_params=params(),
        cost_estimate=pl.CostEstimate(
            flops=2 * len(which) * cap * rows * width, bytes_accessed=10**6, transcendentals=0
        ),
        name="dispatch",
    )(normed, slot_rows, earlier)


def merge_kernel(narrow, which, tokens, own, cached, w_o, gain, router, hits, slot_rows, *refs):
    state_ref, gates_ref, normed_ref = refs[:3]
    count = len(narrow) + len(which)
    out_refs = refs[3 : 3 + count]
    attended, placing = refs[3 + count :]
    for s in range(own.shape[0]):
        part = cached[s].astype(F32)
        lse = part[HD : HD + 1] + part[HD + 1 : HD + 2] + part[HD + 2 : HD + 3]
        m = own[s, HD + EXT : HD + EXT + 1, :]
        total = own[s, HD : HD + 1, :]
        top = jnp.maximum(m, lse)
        w_cached, w_own = jnp.exp2(lse - top), jnp.exp2(m - top)
        norm = 1.0 / (w_cached + w_own * total)
        merged = part[0:HD] * (w_cached * norm) + own[s, 0:HD, :] * (w_own * norm)
        attended[s * HD : (s + 1) * HD, :] = merged.astype(BF16)
    rows_attended = attended[...].T
    fill(out_refs[: len(narrow)], narrow, rows_attended, slot_rows, placing)
    state = tokens[...].astype(F32) + dot(rows_attended, w_o[...])
    state_ref[...] = state
    mean_square = jnp.mean(state * state, axis=-1, keepdims=True)
    normed = (state * lax.rsqrt(mean_square + EPSILON) * gain[...]).astype(BF16)
    logits = dot(normed, router[...])
    squashed = jnp.where(hits[...] > 0, jax.nn.sigmoid(logits), 0.0)
    gates_ref[...] = squashed / jnp.sum(squashed, axis=1, keepdims=True)
    normed_ref[...] = normed
    fill(out_refs[len(narrow) :], which, normed, slot_rows, placing)


def merge_dispatch(tokens, own, cached, w_o, gain, router, hits, slot_rows, narrow, which, cap):
    lanes = own.shape[0]
    rows, width = tokens.shape
    return pl.pallas_call(
        functools.partial(merge_kernel, tuple(narrow), tuple(which)),
        out_shape=[
            jax.ShapeDtypeStruct((rows, width), F32),
            jax.ShapeDtypeStruct((rows, lanes), F32),
            jax.ShapeDtypeStruct((rows, width), BF16),
        ]
        + [jax.ShapeDtypeStruct((cap, lanes * HD), BF16)] * len(narrow)
        + [jax.ShapeDtypeStruct((cap, width), BF16)] * len(which),
        in_specs=vmem(8),
        out_specs=vmem(3 + len(narrow) + len(which)),
        scratch_shapes=[
            pltpu.VMEM((lanes * HD, rows), BF16),
            pltpu.VMEM((max(len(narrow), len(which)) * cap, rows), BF16),
        ],
        compiler_params=params(),
        cost_estimate=pl.CostEstimate(
            flops=4 * 10**9, bytes_accessed=10 * 10**6, transcendentals=10**5
        ),
        name="merge_and_dispatch",
    )(tokens, own, cached, w_o, gain, router, hits, slot_rows)


def expert_kernel(count, late, *refs):
    x_refs = refs[:count]
    if late:
        attended_refs = refs[count : count + late]
        w_o, gain = refs[count + late : count + late + 2]
        refs = refs[late + 2 :]
    gate_ref, up_ref, down_ref = refs[count : count + 3]
    out_refs = refs[count + 4 : 2 * count + 4]
    x_all, total = refs[2 * count + 4 :]
    cap = x_refs[0].shape[0]
    step = pl.program_id(0)

    @pl.when(step == 0)
    def _():
        for n in range(count):
            x = x_refs[n][...]
            if n < late:
                x = rms_norm(x.astype(F32) + dot(attended_refs[n][...], w_o[...]), gain[...])
            x_all[n * cap : (n + 1) * cap, :] = x

    x = x_all[...]
    gate = dot(x, gate_ref[0])
    up = dot(x, up_ref[0])
    active = (jax.nn.gelu(gate, approximate=True) * up).astype(BF16)
    part = dot(active, down_ref[0])

    @pl.when(step == 0)
    def _():
        total[...] = part

    @pl.when(step > 0)
    def _():
        total[...] += part

    @pl.when(step == pl.num_programs(0) - 1)
    def _():
        for n in range(count):
            out_refs[n][...] = total[n * cap : (n + 1) * cap, :].astype(BF16)


def expert(chunks, w_in, w_out, earlier, late=()):
    count = len(chunks)
    cap, width = chunks[0].shape
    hidden = w_out.shape[1]
    tile = 256
    steps = hidden // tile
    whole = pl.BlockSpec((cap, width), lambda j: (0, 0))
    return pl.pallas_call(
        functools.partial(expert_kernel, count, max(0, len(late) - 2)),
        grid=(steps,),
        out_shape=[jax.ShapeDtypeStruct((cap, width), BF16)] * count,
        in_specs=[whole] * count
        + [pl.BlockSpec(extra.shape, lambda j: (0, 0)) for extra in late]
        + [
            pl.BlockSpec((1, width, tile), lambda j: (0, 0, j)),
            pl.BlockSpec((1, width, tile), lambda j: (0, 0, j + steps)),
            pl.BlockSpec((1, tile, width), lambda j: (0, j, 0)),
            pl.BlockSpec(memory_space=pl.ANY),
        ],
        out_specs=[whole] * count,
        scratch_shapes=[
            pltpu.VMEM((count * cap, width), BF16),
            pltpu.VMEM((count * cap, width), F32),
        ],
        compiler_params=params(),
        cost_estimate=pl.CostEstimate(
            flops=6 * count * cap * width * hidden,
            bytes_accessed=6 * width * hidden,
            transcendentals=count * cap * hidden,
        ),
        name="expert",
    )(*chunks, *late, w_in, w_in, w_out, earlier)


def combine_kernel(which, *refs):
    count = len(which)
    base, gates, slots = refs[:3]
    parts = refs[3 : 3 + count]
    out = refs[3 + count]
    rows = base.shape[0]
    cap = parts[0].shape[0]
    total = base[...]
    for n in range(count):
        s = which[n]
        lane = lax.broadcasted_iota(jnp.int32, (rows, cap), 1)
        pick = (lane == slots[:, s : s + 1]).astype(F32).astype(BF16)
        total = total + gates[:, s : s + 1] * dot(pick, parts[n][...])
    out[...] = total.astype(out.dtype)


def combine(base, gates, slots, parts, which, last):
    count = len(parts)
    rows, width = base.shape
    return pl.pallas_call(
        functools.partial(combine_kernel, tuple(which)),
        out_shape=jax.ShapeDtypeStruct((rows, width), BF16 if last else F32),
        in_specs=vmem(3 + count),
        out_specs=pl.BlockSpec(memory_space=pltpu.VMEM),
        compiler_params=params(),
        cost_estimate=pl.CostEstimate(
            flops=2 * count * rows * parts[0].shape[0] * width,
            bytes_accessed=6 * 10**6,
            transcendentals=0,
        ),
        name="combine",
    )(base, gates, slots, *parts)


def body(
    tokens,
    gain_attn,
    w_qkv,
    w_attn_out,
    kv_cache,
    page_table,
    cached_lengths,
    gain_moe,
    w_router,
    routes,
    w_in,
    w_out,
):
    lanes, groups = lax.axis_size("tensor"), lax.axis_size("batch")
    me, group = lax.axis_index("tensor"), lax.axis_index("batch")
    rows, width = tokens.shape
    requests = cached_lengths.shape[0]
    span_devs = lanes // requests
    share = width // groups
    info = jnp.stack([me, group]).astype(jnp.int32)

    w_t = w_qkv.T
    q_high = gather_high(w_t[0:HD], lanes, groups)
    q_plane = gather_plane(q_high, lanes, groups)
    q_other = send(q_plane, lanes, lanes, groups)
    normed = rms_norm(tokens, gain_attn)
    q = project_queries(info, normed, q_plane, q_other)
    q_here = lax.all_to_all(q, "tensor", split_axis=0, concat_axis=0, tiled=True)

    near = [normed]
    rest = jnp.concatenate([w_t[HD : 3 * HD], w_attn_out.T], axis=0)
    ready, rest = lax.optimization_barrier((normed, rest, q))[:2]
    for i in range(1, span_devs):
        pairs = [
            (b * lanes + t, b * lanes + (t ^ i))
            for b in range(groups)
            for t in range(lanes)
            if t % span_devs < (t ^ i) % span_devs
        ]
        near.append(lax.ppermute(ready, AXES, pairs))
    rest = gather_high(rest, lanes, groups)
    rest = gather_plane(after(rest, *near[1:]), lanes, groups)

    names = me ^ jnp.arange(lanes, dtype=jnp.int32)
    hit_rows = (routes[:, 0][None, :] == names[:, None]) | (routes[:, 1][None, :] == names[:, None])
    earlier = jnp.triu(jnp.ones((rows, rows), BF16), 1)
    rank = dot(hit_rows.astype(BF16), earlier).astype(jnp.int32)
    slot_rows = jnp.where(hit_rows, rank, -1)
    slots = slot_rows.T
    hits = hit_rows.astype(jnp.int32).T
    capacity = max(2, (5 * rows * routes.shape[1] + 4 * lanes - 1) // (4 * lanes))
    cap = -(-capacity // 16) * 16
    router = jnp.take(w_router, names, axis=1)

    half = lanes // 2
    near_experts = list(range(half))
    far = [list(range(half, lanes, 2)), list(range(half + 1, lanes, 2))]
    ahead = far[0][: max(1, len(far[0]) // 2)]
    early = dispatch(tokens, slot_rows, ahead, cap, tokens)
    early = lax.optimization_barrier((*early, q_here))[:-1]
    early = [send(part, s, lanes, groups) for s, part in zip(ahead, early)]

    parts = cached_attention(cached_lengths, page_table, q_here, kv_cache)
    rest_other = send(after(rest, parts, *early), lanes, lanes, groups)
    cached = lax.all_to_all(parts, "tensor", split_axis=0, concat_axis=0, tiled=True)
    own, w_o = self_attention(info, q, near, rest, rest_other, parts)

    outcome = merge_dispatch(
        tokens,
        own,
        cached,
        w_o,
        gain_moe.reshape(1, width),
        router,
        hits,
        slot_rows,
        ahead,
        far[0][len(ahead) :] + far[1] + near_experts,
        cap,
    )
    state, gates, normed_moe = outcome[:3]
    late = [send(part, s, lanes, groups) for s, part in zip(ahead, outcome[3:])]
    whole = far[0][len(ahead) :] + far[1] + near_experts
    arrived = dict(zip(whole, outcome[3 + len(ahead) :]))
    arrived.update({s: send(arrived[s], s, lanes, groups) for s in whole if s})
    arrived.update(zip(ahead, early))
    mixed = state
    results = [gates]
    for part in (far[0], near_experts, far[1]):
        more = (*late, w_o, gain_moe.reshape(1, width)) if part is far[0] else ()
        results = expert([arrived[s] for s in part], w_in, w_out, results[0], more)
        returned = [
            results[n] if s == 0 else send(results[n], s, lanes, groups)
            for n, s in enumerate(part)
        ]
        mixed = combine(mixed, gates, slots, returned, part, part is far[1])
    return mixed


def solution(mesh):
    in_specs = (
        P(("batch", "tensor"), None),
        P(),
        P("batch", "tensor"),
        P("batch", "tensor"),
        P("batch", None, "tensor"),
        P("batch", None),
        P("batch"),
        P(),
        P(),
        P(("batch", "tensor"), None),
        P("tensor", None, None),
        P("tensor", None, None),
    )
    out_specs = P(("batch", "tensor"), None)
    return jax.shard_map(body, mesh=mesh, in_specs=in_specs, out_specs=out_specs, check_vma=False)
```

```python
import functools
import math

import jax
import jax.numpy as jnp
from jax import lax
from jax.experimental import pallas as pl
from jax.experimental.pallas import tpu as pltpu
from jax.sharding import PartitionSpec as P

HD = 64
EXT = 16
EPSILON = 1e-06
NEGATIVE = -1e30
F32, BF16 = jnp.float32, jnp.bfloat16
NT = (((1,), (1,)), ((), ()))
VMEM_LIMIT = 52 * 1024 * 1024
AXES = ("batch", "tensor")


def dot(a, b, dims=(((1,), (0,)), ((), ()))):
    return lax.dot_general(a, b, dims, preferred_element_type=F32)


def rms_norm(values, gain):
    values = values.astype(F32)
    mean_square = jnp.mean(values * values, axis=-1, keepdims=True)
    return (values * lax.rsqrt(mean_square + EPSILON) * gain).astype(BF16)


def vmem(count):
    return [pl.BlockSpec(memory_space=pltpu.VMEM)] * count


def smem(count):
    return [pl.BlockSpec(memory_space=pltpu.SMEM)] * count


def params():
    return pltpu.CompilerParams(vmem_limit_bytes=VMEM_LIMIT)


def send(value, mask, lanes, groups):
    total = lanes * groups
    return lax.ppermute(value, AXES, [(i, i ^ mask) for i in range(total)])


def gather_high(piece, lanes, groups):
    low = max(1, lanes // 4)
    return jnp.stack([piece] + [send(piece, s, lanes, groups) for s in range(low, lanes, low)])


def gather_plane(block, lanes, groups):
    low = max(1, lanes // 4)
    rows = []
    for j in range(0, groups, 2):
        masks = [j * lanes + s for s in range(low)]
        rows.append(
            jnp.stack([send(block, m, lanes, groups) if m else block for m in masks], axis=1)
        )
    return jnp.stack(rows).reshape((groups // 2, lanes) + block.shape[1:])


def after(value, *others):
    return lax.optimization_barrier((value,) + others)[0]


def ones_rows(keys):
    return jnp.ones((EXT, keys), BF16)


def softmax_steps(scores, values, old):
    tops = [jnp.maximum(m, jnp.max(s, axis=0, keepdims=True)) for s, (m, acc) in zip(scores, old)]
    return [
        (top, acc * jnp.exp2(m - top) + dot(v, jnp.exp2(s - top).astype(BF16)))
        for s, v, top, (m, acc) in zip(scores, values, tops, old)
    ]


def cached_kernel(requests, span_devs, block_pages, lengths, table, q_ref, kv_ref, out_ref, q_all, m_ref, acc_ref):
    page = kv_ref.shape[1]
    pages = table.shape[1] // requests
    rows = q_ref.shape[2]
    queries = rows * span_devs
    keys = block_pages * page
    tile = min(256, queries)
    tiles = [slice(t, t + tile) for t in range(0, queries, tile)]
    q_all[HD : 2 * HD, :] = jnp.zeros((HD, queries), BF16)

    def one_request(request, carry):
        length = lengths[request]
        for i in range(span_devs):
            q_all[0:HD, i * rows : (i + 1) * rows] = q_ref[request * span_devs + i]
        m_ref[...] = jnp.full((1, queries), NEGATIVE, F32)
        acc_ref[...] = jnp.zeros((HD + EXT, queries), F32)

        def block(j, masked):
            parts = [
                kv_ref[
                    table[0, request * pages + jnp.minimum(j * block_pages + n, pages - 1)]
                ]
                for n in range(block_pages)
            ]
            both = jnp.concatenate(parts, axis=0)
            values = jnp.concatenate([both.T[HD : 2 * HD], ones_rows(keys)], axis=0)
            scores = [dot(both, q_all[:, at]) for at in tiles]
            if masked:
                position = j * keys + lax.broadcasted_iota(jnp.int32, scores[0].shape, 0)
                scores = [jnp.where(position < length, s, NEGATIVE) for s in scores]
            old = [(m_ref[:, at], acc_ref[:, at]) for at in tiles]
            new = softmax_steps(scores, [values] * len(tiles), old)
            for at, (top, acc) in zip(tiles, new):
                m_ref[:, at] = top
                acc_ref[:, at] = acc

        whole = length // keys

        def step(j, c):
            block(j, False)
            return c

        lax.fori_loop(0, whole, step, 0)

        @pl.when(whole * keys < length)
        def _():
            block(whole, True)

        total = acc_ref[HD : HD + 1, :]
        lse = m_ref[...] + jnp.log2(total)
        hi = lse.astype(BF16).astype(F32)
        mid = (lse - hi).astype(BF16).astype(F32)
        lo = lse - hi - mid
        at_row = lax.broadcasted_iota(jnp.int32, (EXT, queries), 0)
        stats = jnp.where(
            at_row == 0, hi, jnp.where(at_row == 1, mid, jnp.where(at_row == 2, lo, 0.0))
        ).astype(BF16)
        values = (acc_ref[0:HD, :] * (1.0 / total)).astype(BF16)
        for i in range(span_devs):
            at = slice(i * rows, (i + 1) * rows)
            out_ref[request * span_devs + i, 0:HD, :] = values[:, at]
            out_ref[request * span_devs + i, HD : HD + EXT, :] = stats[:, at]
        return carry

    lax.fori_loop(0, requests, one_request, 0)


def cached_attention(lengths, table, q, kv_cache):
    lanes, _, rows = q.shape
    requests = lengths.shape[0]
    span_devs = lanes // requests
    queries = rows * span_devs
    return pl.pallas_call(
        functools.partial(cached_kernel, requests, span_devs, 4),
        out_shape=jax.ShapeDtypeStruct((lanes, HD + EXT, rows), BF16),
        in_specs=smem(2) + vmem(2),
        out_specs=pl.BlockSpec(memory_space=pltpu.VMEM),
        scratch_shapes=[
            pltpu.VMEM((2 * HD, queries), BF16),
            pltpu.VMEM((1, queries), F32),
            pltpu.VMEM((HD + EXT, queries), F32),
        ],
        compiler_params=params(),
        cost_estimate=pl.CostEstimate(
            flops=24 * 10**9, bytes_accessed=6 * 10**6, transcendentals=8 * 10**6
        ),
        name="cached_attention",
    )(lengths, table, q, kv_cache)


def query_kernel(scale, info, normed, even, odd, out_ref):
    lanes, _, rows = out_ref.shape
    halves, _, _, share = even.shape
    total = jnp.zeros((lanes * HD, rows), F32)
    for n in range(halves):
        for low, ref in enumerate((even, odd)):
            at = jnp.bitwise_xor(info[1], 2 * n + low) * share
            columns = normed[:, pl.ds(pl.multiple_of(at, share), share)]
            total = total + dot(ref[n].reshape(lanes * HD, share), columns, NT)
    q = (total * scale).astype(BF16)
    for s in range(lanes):
        out_ref[jnp.bitwise_xor(info[0], s)] = q[s * HD : (s + 1) * HD]


def project_queries(info, normed, even, odd):
    lanes = even.shape[1]
    rows = normed.shape[0]
    scale = math.log2(math.e) / math.sqrt(HD)
    return pl.pallas_call(
        functools.partial(query_kernel, scale),
        out_shape=jax.ShapeDtypeStruct((lanes, HD, rows), BF16),
        in_specs=smem(1) + vmem(3),
        out_specs=pl.BlockSpec(memory_space=pltpu.VMEM),
        compiler_params=params(),
        cost_estimate=pl.CostEstimate(flops=10**9, bytes_accessed=2 * 10**6, transcendentals=0),
        name="project_queries",
    )(info, normed, even, odd)


def self_kernel(span_devs, *refs):
    info, q_ref = refs[:2]
    normed_refs = refs[2 : 2 + span_devs]
    even, odd = refs[2 + span_devs : 4 + span_devs]
    out_ref, w_o_ref, w_k, w_v, keys_ref, values_ref = refs[5 + span_devs :]
    lanes, _, rows = q_ref.shape
    halves, _, _, share = even.shape
    groups = 2 * halves
    me, group = info[0], info[1]
    at = me % span_devs

    for n in range(halves):
        for low, ref in enumerate((even, odd)):
            column = pl.ds(
                pl.multiple_of(jnp.bitwise_xor(group, 2 * n + low) * share, share), share
            )
            for h in range(lanes):
                piece = ref[n, jnp.bitwise_xor(me, h)]
                head = slice(h * HD, (h + 1) * HD)
                w_k[head, column] = piece[0:HD]
                w_v[head, column] = piece[HD : 2 * HD]
                w_o_ref[head, column] = piece[2 * HD : 3 * HD]

    def project(normed):
        keys_ref[...] = dot(normed[...], w_k[...], NT).astype(BF16)
        values_ref[...] = dot(w_v[...], normed[...], NT).astype(BF16)

    together = 4
    tile = min(256, rows)

    def run(causal):
        def step(g, carry):
            scores, values, old, places = [], [], [], []
            nothing = jnp.zeros((HD, tile), BF16)
            for p in range(together // 2):
                block = pl.multiple_of((g * together + 2 * p) * HD, 2 * HD)
                keys = keys_ref[:, pl.ds(block, 2 * HD)]
                both_v = values_ref[pl.ds(block, 2 * HD), :]
                for h in range(2):
                    s = g * together + 2 * p + h
                    q = q_ref[s]
                    value = jnp.concatenate([both_v[h * HD : (h + 1) * HD], ones_rows(rows)], axis=0)
                    for t in range(0, rows, tile):
                        here = slice(t, t + tile)
                        seen = t + tile if causal else rows
                        part = [nothing, q[:, here]] if h else [q[:, here], nothing]
                        score = dot(keys[0:seen], jnp.concatenate(part, axis=0))
                        if causal:
                            position = lax.broadcasted_iota(jnp.int32, score.shape, 0)
                            line = t + lax.broadcasted_iota(jnp.int32, score.shape, 1)
                            score = jnp.where(position <= line, score, NEGATIVE)
                            m = jnp.full((1, tile), NEGATIVE, F32)
                            acc = jnp.zeros((HD + EXT, tile), F32)
                        else:
                            m = out_ref[s, HD + EXT : HD + EXT + 1, here]
                            acc = out_ref[s, 0 : HD + EXT, here]
                        scores.append(score)
                        values.append(value[:, 0:seen])
                        old.append((m, acc))
                        places.append((s, here))
            for (s, here), (top, acc) in zip(places, softmax_steps(scores, values, old)):
                out_ref[s, 0 : HD + EXT, here] = acc
                out_ref[s, HD + EXT : HD + EXT + 8, here] = jnp.broadcast_to(top, (8, tile))
            return carry

        lax.fori_loop(0, lanes // together, step, 0)

    project(normed_refs[0])
    run(True)
    for other in range(1, span_devs):

        @pl.when(jnp.bitwise_xor(at, other) < at)
        def _(other=other):
            project(normed_refs[other])
            run(False)


def self_attention(info, q, normed, even, odd, earlier):
    span_devs = len(normed)
    lanes, _, rows = q.shape
    width = normed[0].shape[1]
    anywhere = [pl.BlockSpec(memory_space=pl.ANY)]
    return pl.pallas_call(
        functools.partial(self_kernel, span_devs),
        out_shape=[
            jax.ShapeDtypeStruct((lanes, HD + EXT + 8, rows), F32),
            jax.ShapeDtypeStruct((lanes * HD, width), BF16),
        ],
        in_specs=smem(1) + vmem(3 + span_devs) + anywhere,
        out_specs=vmem(2),
        scratch_shapes=[
            pltpu.VMEM((lanes * HD, width), BF16),
            pltpu.VMEM((lanes * HD, width), BF16),
            pltpu.VMEM((rows, lanes * HD), BF16),
            pltpu.VMEM((lanes * HD, rows), BF16),
        ],
        compiler_params=params(),
        cost_estimate=pl.CostEstimate(
            flops=4 * 10**9, bytes_accessed=5 * 10**6, transcendentals=4 * 10**6
        ),
        name="self_attention",
    )(info, q, *normed, even, odd, earlier)


def fill(out_refs, which, values, slot_rows, placing):
    cap = out_refs[0].shape[0]
    rows = values.shape[0]
    for n, s in enumerate(which):
        at_slot = lax.broadcasted_iota(jnp.int32, (cap, rows), 0)
        placing[n * cap : (n + 1) * cap, :] = (
            (at_slot == slot_rows[s : s + 1, :]).astype(F32).astype(BF16)
        )
    rows_out = dot(placing[0 : len(which) * cap, :], values).astype(BF16)
    for n in range(len(which)):
        out_refs[n][...] = rows_out[n * cap : (n + 1) * cap, :]


def dispatch_kernel(which, *refs):
    normed, slot_rows = refs[:2]
    out_refs = refs[3 : 3 + len(which)]
    fill(out_refs, which, normed[...], slot_rows, refs[3 + len(which)])


def dispatch(normed, slot_rows, which, cap, earlier):
    rows, width = normed.shape
    return pl.pallas_call(
        functools.partial(dispatch_kernel, tuple(which)),
        out_shape=[jax.ShapeDtypeStruct((cap, width), BF16)] * len(which),
        in_specs=vmem(2) + [pl.BlockSpec(memory_space=pl.ANY)],
        out_specs=vmem(len(which)),
        scratch_shapes=[pltpu.VMEM((len(which) * cap, rows), BF16)],
        compiler_params=params(),
        cost_estimate=pl.CostEstimate(
            flops=2 * len(which) * cap * rows * width, bytes_accessed=10**6, transcendentals=0
        ),
        name="dispatch",
    )(normed, slot_rows, earlier)


def merge_kernel(narrow, which, tokens, own, cached, w_o, gain, router, hits, slot_rows, *refs):
    state_ref, gates_ref, normed_ref = refs[:3]
    count = len(narrow) + len(which)
    out_refs = refs[3 : 3 + count]
    attended, placing = refs[3 + count :]
    for s in range(own.shape[0]):
        part = cached[s].astype(F32)
        lse = part[HD : HD + 1] + part[HD + 1 : HD + 2] + part[HD + 2 : HD + 3]
        m = own[s, HD + EXT : HD + EXT + 1, :]
        total = own[s, HD : HD + 1, :]
        top = jnp.maximum(m, lse)
        w_cached, w_own = jnp.exp2(lse - top), jnp.exp2(m - top)
        norm = 1.0 / (w_cached + w_own * total)
        merged = part[0:HD] * (w_cached * norm) + own[s, 0:HD, :] * (w_own * norm)
        attended[s * HD : (s + 1) * HD, :] = merged.astype(BF16)
    rows_attended = attended[...].T
    fill(out_refs[: len(narrow)], narrow, rows_attended, slot_rows, placing)
    state = tokens[...].astype(F32) + dot(rows_attended, w_o[...])
    state_ref[...] = state
    mean_square = jnp.mean(state * state, axis=-1, keepdims=True)
    normed = (state * lax.rsqrt(mean_square + EPSILON) * gain[...]).astype(BF16)
    logits = dot(normed, router[...])
    squashed = jnp.where(hits[...] > 0, jax.nn.sigmoid(logits), 0.0)
    gates_ref[...] = squashed / jnp.sum(squashed, axis=1, keepdims=True)
    normed_ref[...] = normed
    fill(out_refs[len(narrow) :], which, normed, slot_rows, placing)


def merge_dispatch(tokens, own, cached, w_o, gain, router, hits, slot_rows, narrow, which, cap):
    lanes = own.shape[0]
    rows, width = tokens.shape
    return pl.pallas_call(
        functools.partial(merge_kernel, tuple(narrow), tuple(which)),
        out_shape=[
            jax.ShapeDtypeStruct((rows, width), F32),
            jax.ShapeDtypeStruct((rows, lanes), F32),
            jax.ShapeDtypeStruct((rows, width), BF16),
        ]
        + [jax.ShapeDtypeStruct((cap, lanes * HD), BF16)] * len(narrow)
        + [jax.ShapeDtypeStruct((cap, width), BF16)] * len(which),
        in_specs=vmem(8),
        out_specs=vmem(3 + len(narrow) + len(which)),
        scratch_shapes=[
            pltpu.VMEM((lanes * HD, rows), BF16),
            pltpu.VMEM((max(len(narrow), len(which)) * cap, rows), BF16),
        ],
        compiler_params=params(),
        cost_estimate=pl.CostEstimate(
            flops=4 * 10**9, bytes_accessed=10 * 10**6, transcendentals=10**5
        ),
        name="merge_and_dispatch",
    )(tokens, own, cached, w_o, gain, router, hits, slot_rows)


def expert_kernel(count, late, *refs):
    x_refs = refs[:count]
    if late:
        attended_refs = refs[count : count + late]
        w_o, gain = refs[count + late : count + late + 2]
        refs = refs[late + 2 :]
    gate_ref, up_ref, down_ref = refs[count : count + 3]
    out_refs = refs[count + 4 : 2 * count + 4]
    x_all, total = refs[2 * count + 4 :]
    cap = x_refs[0].shape[0]
    step = pl.program_id(0)

    @pl.when(step == 0)
    def _():
        for n in range(count):
            x = x_refs[n][...]
            if n < late:
                x = rms_norm(x.astype(F32) + dot(attended_refs[n][...], w_o[...]), gain[...])
            x_all[n * cap : (n + 1) * cap, :] = x

    x = x_all[...]
    gate = dot(x, gate_ref[0])
    up = dot(x, up_ref[0])
    active = (jax.nn.gelu(gate, approximate=True) * up).astype(BF16)
    part = dot(active, down_ref[0])

    @pl.when(step == 0)
    def _():
        total[...] = part

    @pl.when(step > 0)
    def _():
        total[...] += part

    @pl.when(step == pl.num_programs(0) - 1)
    def _():
        for n in range(count):
            out_refs[n][...] = total[n * cap : (n + 1) * cap, :].astype(BF16)


def expert(chunks, w_in, w_out, earlier, late=()):
    count = len(chunks)
    cap, width = chunks[0].shape
    hidden = w_out.shape[1]
    tile = 256
    steps = hidden // tile
    whole = pl.BlockSpec((cap, width), lambda j: (0, 0))
    return pl.pallas_call(
        functools.partial(expert_kernel, count, max(0, len(late) - 2)),
        grid=(steps,),
        out_shape=[jax.ShapeDtypeStruct((cap, width), BF16)] * count,
        in_specs=[whole] * count
        + [pl.BlockSpec(extra.shape, lambda j: (0, 0)) for extra in late]
        + [
            pl.BlockSpec((1, width, tile), lambda j: (0, 0, j)),
            pl.BlockSpec((1, width, tile), lambda j: (0, 0, j + steps)),
            pl.BlockSpec((1, tile, width), lambda j: (0, j, 0)),
            pl.BlockSpec(memory_space=pl.ANY),
        ],
        out_specs=[whole] * count,
        scratch_shapes=[
            pltpu.VMEM((count * cap, width), BF16),
            pltpu.VMEM((count * cap, width), F32),
        ],
        compiler_params=params(),
        cost_estimate=pl.CostEstimate(
            flops=6 * count * cap * width * hidden,
            bytes_accessed=6 * width * hidden,
            transcendentals=count * cap * hidden,
        ),
        name="expert",
    )(*chunks, *late, w_in, w_in, w_out, earlier)


def combine_kernel(which, *refs):
    count = len(which)
    base, gates, slots = refs[:3]
    parts = refs[3 : 3 + count]
    out = refs[3 + count]
    rows = base.shape[0]
    cap = parts[0].shape[0]
    total = base[...]
    for n in range(count):
        s = which[n]
        lane = lax.broadcasted_iota(jnp.int32, (rows, cap), 1)
        pick = (lane == slots[:, s : s + 1]).astype(F32).astype(BF16)
        total = total + gates[:, s : s + 1] * dot(pick, parts[n][...])
    out[...] = total.astype(out.dtype)


def combine(base, gates, slots, parts, which, last):
    count = len(parts)
    rows, width = base.shape
    return pl.pallas_call(
        functools.partial(combine_kernel, tuple(which)),
        out_shape=jax.ShapeDtypeStruct((rows, width), BF16 if last else F32),
        in_specs=vmem(3 + count),
        out_specs=pl.BlockSpec(memory_space=pltpu.VMEM),
        compiler_params=params(),
        cost_estimate=pl.CostEstimate(
            flops=2 * count * rows * parts[0].shape[0] * width,
            bytes_accessed=6 * 10**6,
            transcendentals=0,
        ),
        name="combine",
    )(base, gates, slots, *parts)


def body(
    tokens,
    gain_attn,
    w_qkv,
    w_attn_out,
    kv_cache,
    page_table,
    cached_lengths,
    gain_moe,
    w_router,
    routes,
    w_in,
    w_out,
):
    lanes, groups = lax.axis_size("tensor"), lax.axis_size("batch")
    me, group = lax.axis_index("tensor"), lax.axis_index("batch")
    rows, width = tokens.shape
    requests = cached_lengths.shape[0]
    span_devs = lanes // requests
    share = width // groups
    info = jnp.stack([me, group]).astype(jnp.int32)

    w_t = w_qkv.T
    q_high = gather_high(w_t[0:HD], lanes, groups)
    q_plane = gather_plane(q_high, lanes, groups)
    q_other = send(q_plane, lanes, lanes, groups)
    normed = rms_norm(tokens, gain_attn)
    q = project_queries(info, normed, q_plane, q_other)
    q_here = lax.all_to_all(q, "tensor", split_axis=0, concat_axis=0, tiled=True)

    near = [normed]
    rest = jnp.concatenate([w_t[HD : 3 * HD], w_attn_out.T], axis=0)
    ready, rest = after(normed, q_plane), after(rest, q)
    for i in range(1, span_devs):
        pairs = [
            (b * lanes + t, b * lanes + (t ^ i))
            for b in range(groups)
            for t in range(lanes)
            if t % span_devs < (t ^ i) % span_devs
        ]
        near.append(lax.ppermute(ready, AXES, pairs))
    rest = gather_high(rest, lanes, groups)
    rest = gather_plane(after(rest, q_here, *near[1:]), lanes, groups)

    names = me ^ jnp.arange(lanes, dtype=jnp.int32)
    hit_rows = (routes[:, 0][None, :] == names[:, None]) | (routes[:, 1][None, :] == names[:, None])
    earlier = jnp.triu(jnp.ones((rows, rows), BF16), 1)
    rank = dot(hit_rows.astype(BF16), earlier).astype(jnp.int32)
    slot_rows = jnp.where(hit_rows, rank, -1)
    slots = slot_rows.T
    hits = hit_rows.astype(jnp.int32).T
    capacity = max(2, (5 * rows * routes.shape[1] + 4 * lanes - 1) // (4 * lanes))
    cap = -(-capacity // 16) * 16
    router = jnp.take(w_router, names, axis=1)

    half = lanes // 2
    near_experts = list(range(half))
    far = [list(range(half, lanes, 2)), list(range(half + 1, lanes, 2))]
    ahead = far[0][: max(1, len(far[0]) // 2)]
    early = dispatch(tokens, slot_rows, ahead, cap, tokens)
    early = lax.optimization_barrier((*early, q_here))[:-1]
    early = [send(part, s, lanes, groups) for s, part in zip(ahead, early)]

    parts = cached_attention(cached_lengths, page_table, q_here, kv_cache)
    rest_other = send(after(rest, parts, *early), lanes, lanes, groups)
    cached = lax.all_to_all(parts, "tensor", split_axis=0, concat_axis=0, tiled=True)
    own, w_o = self_attention(info, q, near, rest, rest_other, parts)

    outcome = merge_dispatch(
        tokens,
        own,
        cached,
        w_o,
        gain_moe.reshape(1, width),
        router,
        hits,
        slot_rows,
        ahead,
        far[0][len(ahead) :] + far[1] + near_experts,
        cap,
    )
    state, gates, normed_moe = outcome[:3]
    late = [send(part, s, lanes, groups) for s, part in zip(ahead, outcome[3:])]
    whole = far[0][len(ahead) :] + far[1] + near_experts
    arrived = dict(zip(whole, outcome[3 + len(ahead) :]))
    arrived.update({s: send(arrived[s], s, lanes, groups) for s in whole if s})
    arrived.update(zip(ahead, early))
    mixed = state
    results = [gates]
    for part in (far[0], near_experts, far[1]):
        more = (*late, w_o, gain_moe.reshape(1, width)) if part is far[0] else ()
        results = expert([arrived[s] for s in part], w_in, w_out, results[0], more)
        returned = [
            results[n] if s == 0 else send(results[n], s, lanes, groups)
            for n, s in enumerate(part)
        ]
        mixed = combine(mixed, gates, slots, returned, part, part is far[1])
    return mixed


def solution(mesh):
    in_specs = (
        P(("batch", "tensor"), None),
        P(),
        P("batch", "tensor"),
        P("batch", "tensor"),
        P("batch", None, "tensor"),
        P("batch", None),
        P("batch"),
        P(),
        P(),
        P(("batch", "tensor"), None),
        P("tensor", None, None),
        P("tensor", None, None),
    )
    out_specs = P(("batch", "tensor"), None)
    return jax.shard_map(body, mesh=mesh, in_specs=in_specs, out_specs=out_specs, check_vma=False)
```

```python
import functools
import math

import jax
import jax.numpy as jnp
from jax import lax
from jax.experimental import pallas as pl
from jax.experimental.pallas import tpu as pltpu
from jax.sharding import PartitionSpec as P

HD = 64
EXT = 16
EPSILON = 1e-06
NEGATIVE = -1e30
F32, BF16 = jnp.float32, jnp.bfloat16
NT = (((1,), (1,)), ((), ()))
VMEM_LIMIT = 52 * 1024 * 1024
AXES = ("batch", "tensor")


def dot(a, b, dims=(((1,), (0,)), ((), ()))):
    return lax.dot_general(a, b, dims, preferred_element_type=F32)


def rms_norm(values, gain):
    values = values.astype(F32)
    mean_square = jnp.mean(values * values, axis=-1, keepdims=True)
    return (values * lax.rsqrt(mean_square + EPSILON) * gain).astype(BF16)


def vmem(count):
    return [pl.BlockSpec(memory_space=pltpu.VMEM)] * count


def smem(count):
    return [pl.BlockSpec(memory_space=pltpu.SMEM)] * count


def params():
    return pltpu.CompilerParams(vmem_limit_bytes=VMEM_LIMIT)


def send(value, mask, lanes, groups):
    total = lanes * groups
    return lax.ppermute(value, AXES, [(i, i ^ mask) for i in range(total)])


def gather_high(piece, lanes, groups):
    low = max(1, lanes // 4)
    return jnp.stack([piece] + [send(piece, s, lanes, groups) for s in range(low, lanes, low)])


def gather_plane(block, lanes, groups):
    low = max(1, lanes // 4)
    rows = []
    for j in range(0, groups, 2):
        masks = [j * lanes + s for s in range(low)]
        rows.append(
            jnp.stack([send(block, m, lanes, groups) if m else block for m in masks], axis=1)
        )
    return jnp.stack(rows).reshape((groups // 2, lanes) + block.shape[1:])


def after(value, *others):
    return lax.optimization_barrier((value,) + others)[0]


def ones_rows(keys):
    return jnp.ones((EXT, keys), BF16)


def softmax_steps(scores, values, old):
    tops = [jnp.maximum(m, jnp.max(s, axis=0, keepdims=True)) for s, (m, acc) in zip(scores, old)]
    return [
        (top, acc * jnp.exp2(m - top) + dot(v, jnp.exp2(s - top).astype(BF16)))
        for s, v, top, (m, acc) in zip(scores, values, tops, old)
    ]


def cached_kernel(requests, span_devs, block_pages, lengths, table, q_ref, kv_ref, out_ref, q_all, m_ref, acc_ref):
    page = kv_ref.shape[1]
    pages = table.shape[1] // requests
    rows = q_ref.shape[2]
    queries = rows * span_devs
    keys = block_pages * page
    tile = min(256, queries)
    tiles = [slice(t, t + tile) for t in range(0, queries, tile)]
    q_all[HD : 2 * HD, :] = jnp.zeros((HD, queries), BF16)

    def one_request(request, carry):
        length = lengths[request]
        for i in range(span_devs):
            q_all[0:HD, i * rows : (i + 1) * rows] = q_ref[request * span_devs + i]
        m_ref[...] = jnp.full((1, queries), NEGATIVE, F32)
        acc_ref[...] = jnp.zeros((HD + EXT, queries), F32)

        def block(j, masked):
            parts = [
                kv_ref[
                    table[0, request * pages + jnp.minimum(j * block_pages + n, pages - 1)]
                ]
                for n in range(block_pages)
            ]
            both = jnp.concatenate(parts, axis=0)
            values = jnp.concatenate([both.T[HD : 2 * HD], ones_rows(keys)], axis=0)
            scores = [dot(both, q_all[:, at]) for at in tiles]
            if masked:
                position = j * keys + lax.broadcasted_iota(jnp.int32, scores[0].shape, 0)
                scores = [jnp.where(position < length, s, NEGATIVE) for s in scores]
            old = [(m_ref[:, at], acc_ref[:, at]) for at in tiles]
            new = softmax_steps(scores, [values] * len(tiles), old)
            for at, (top, acc) in zip(tiles, new):
                m_ref[:, at] = top
                acc_ref[:, at] = acc

        whole = length // keys

        def step(j, c):
            block(j, False)
            return c

        lax.fori_loop(0, whole, step, 0)

        @pl.when(whole * keys < length)
        def _():
            block(whole, True)

        total = acc_ref[HD : HD + 1, :]
        lse = m_ref[...] + jnp.log2(total)
        hi = lse.astype(BF16).astype(F32)
        mid = (lse - hi).astype(BF16).astype(F32)
        lo = lse - hi - mid
        at_row = lax.broadcasted_iota(jnp.int32, (EXT, queries), 0)
        stats = jnp.where(
            at_row == 0, hi, jnp.where(at_row == 1, mid, jnp.where(at_row == 2, lo, 0.0))
        ).astype(BF16)
        values = (acc_ref[0:HD, :] * (1.0 / total)).astype(BF16)
        for i in range(span_devs):
            at = slice(i * rows, (i + 1) * rows)
            out_ref[request * span_devs + i, 0:HD, :] = values[:, at]
            out_ref[request * span_devs + i, HD : HD + EXT, :] = stats[:, at]
        return carry

    lax.fori_loop(0, requests, one_request, 0)


def cached_attention(lengths, table, q, kv_cache):
    lanes, _, rows = q.shape
    requests = lengths.shape[0]
    span_devs = lanes // requests
    queries = rows * span_devs
    return pl.pallas_call(
        functools.partial(cached_kernel, requests, span_devs, 8),
        out_shape=jax.ShapeDtypeStruct((lanes, HD + EXT, rows), BF16),
        in_specs=smem(2) + vmem(2),
        out_specs=pl.BlockSpec(memory_space=pltpu.VMEM),
        scratch_shapes=[
            pltpu.VMEM((2 * HD, queries), BF16),
            pltpu.VMEM((1, queries), F32),
            pltpu.VMEM((HD + EXT, queries), F32),
        ],
        compiler_params=params(),
        cost_estimate=pl.CostEstimate(
            flops=24 * 10**9, bytes_accessed=6 * 10**6, transcendentals=8 * 10**6
        ),
        name="cached_attention",
    )(lengths, table, q, kv_cache)


def query_kernel(scale, info, normed, even, odd, out_ref):
    lanes, _, rows = out_ref.shape
    halves, _, _, share = even.shape
    total = jnp.zeros((lanes * HD, rows), F32)
    for n in range(halves):
        for low, ref in enumerate((even, odd)):
            at = jnp.bitwise_xor(info[1], 2 * n + low) * share
            columns = normed[:, pl.ds(pl.multiple_of(at, share), share)]
            total = total + dot(ref[n].reshape(lanes * HD, share), columns, NT)
    q = (total * scale).astype(BF16)
    for s in range(lanes):
        out_ref[jnp.bitwise_xor(info[0], s)] = q[s * HD : (s + 1) * HD]


def project_queries(info, normed, even, odd):
    lanes = even.shape[1]
    rows = normed.shape[0]
    scale = math.log2(math.e) / math.sqrt(HD)
    return pl.pallas_call(
        functools.partial(query_kernel, scale),
        out_shape=jax.ShapeDtypeStruct((lanes, HD, rows), BF16),
        in_specs=smem(1) + vmem(3),
        out_specs=pl.BlockSpec(memory_space=pltpu.VMEM),
        compiler_params=params(),
        cost_estimate=pl.CostEstimate(flops=10**9, bytes_accessed=2 * 10**6, transcendentals=0),
        name="project_queries",
    )(info, normed, even, odd)


def self_kernel(span_devs, *refs):
    info, q_ref = refs[:2]
    normed_refs = refs[2 : 2 + span_devs]
    even, odd = refs[2 + span_devs : 4 + span_devs]
    out_ref, w_o_ref, w_k, w_v, keys_ref, values_ref = refs[5 + span_devs :]
    lanes, _, rows = q_ref.shape
    halves, _, _, share = even.shape
    groups = 2 * halves
    me, group = info[0], info[1]
    at = me % span_devs

    for n in range(halves):
        for low, ref in enumerate((even, odd)):
            column = pl.ds(
                pl.multiple_of(jnp.bitwise_xor(group, 2 * n + low) * share, share), share
            )
            for h in range(lanes):
                piece = ref[n, jnp.bitwise_xor(me, h)]
                head = slice(h * HD, (h + 1) * HD)
                w_k[head, column] = piece[0:HD]
                w_v[head, column] = piece[HD : 2 * HD]
                w_o_ref[head, column] = piece[2 * HD : 3 * HD]

    def project(normed):
        keys_ref[...] = dot(normed[...], w_k[...], NT).astype(BF16)
        values_ref[...] = dot(w_v[...], normed[...], NT).astype(BF16)

    together = 4
    tile = min(256, rows)

    def run(causal):
        def step(g, carry):
            scores, values, old, places = [], [], [], []
            nothing = jnp.zeros((HD, tile), BF16)
            for p in range(together // 2):
                block = pl.multiple_of((g * together + 2 * p) * HD, 2 * HD)
                keys = keys_ref[:, pl.ds(block, 2 * HD)]
                both_v = values_ref[pl.ds(block, 2 * HD), :]
                for h in range(2):
                    s = g * together + 2 * p + h
                    q = q_ref[s]
                    value = jnp.concatenate([both_v[h * HD : (h + 1) * HD], ones_rows(rows)], axis=0)
                    for t in range(0, rows, tile):
                        here = slice(t, t + tile)
                        seen = t + tile if causal else rows
                        part = [nothing, q[:, here]] if h else [q[:, here], nothing]
                        score = dot(keys[0:seen], jnp.concatenate(part, axis=0))
                        if causal:
                            position = lax.broadcasted_iota(jnp.int32, score.shape, 0)
                            line = t + lax.broadcasted_iota(jnp.int32, score.shape, 1)
                            score = jnp.where(position <= line, score, NEGATIVE)
                            m = jnp.full((1, tile), NEGATIVE, F32)
                            acc = jnp.zeros((HD + EXT, tile), F32)
                        else:
                            m = out_ref[s, HD + EXT : HD + EXT + 1, here]
                            acc = out_ref[s, 0 : HD + EXT, here]
                        scores.append(score)
                        values.append(value[:, 0:seen])
                        old.append((m, acc))
                        places.append((s, here))
            for (s, here), (top, acc) in zip(places, softmax_steps(scores, values, old)):
                out_ref[s, 0 : HD + EXT, here] = acc
                out_ref[s, HD + EXT : HD + EXT + 8, here] = jnp.broadcast_to(top, (8, tile))
            return carry

        lax.fori_loop(0, lanes // together, step, 0)

    project(normed_refs[0])
    run(True)
    for other in range(1, span_devs):

        @pl.when(jnp.bitwise_xor(at, other) < at)
        def _(other=other):
            project(normed_refs[other])
            run(False)


def self_attention(info, q, normed, even, odd, earlier):
    span_devs = len(normed)
    lanes, _, rows = q.shape
    width = normed[0].shape[1]
    anywhere = [pl.BlockSpec(memory_space=pl.ANY)]
    return pl.pallas_call(
        functools.partial(self_kernel, span_devs),
        out_shape=[
            jax.ShapeDtypeStruct((lanes, HD + EXT + 8, rows), F32),
            jax.ShapeDtypeStruct((lanes * HD, width), BF16),
        ],
        in_specs=smem(1) + vmem(3 + span_devs) + anywhere,
        out_specs=vmem(2),
        scratch_shapes=[
            pltpu.VMEM((lanes * HD, width), BF16),
            pltpu.VMEM((lanes * HD, width), BF16),
            pltpu.VMEM((rows, lanes * HD), BF16),
            pltpu.VMEM((lanes * HD, rows), BF16),
        ],
        compiler_params=params(),
        cost_estimate=pl.CostEstimate(
            flops=4 * 10**9, bytes_accessed=5 * 10**6, transcendentals=4 * 10**6
        ),
        name="self_attention",
    )(info, q, *normed, even, odd, earlier)


def fill(out_refs, which, values, slot_rows, placing):
    cap = out_refs[0].shape[0]
    rows = values.shape[0]
    for n, s in enumerate(which):
        at_slot = lax.broadcasted_iota(jnp.int32, (cap, rows), 0)
        placing[n * cap : (n + 1) * cap, :] = (
            (at_slot == slot_rows[s : s + 1, :]).astype(F32).astype(BF16)
        )
    rows_out = dot(placing[0 : len(which) * cap, :], values).astype(BF16)
    for n in range(len(which)):
        out_refs[n][...] = rows_out[n * cap : (n + 1) * cap, :]


def dispatch_kernel(which, *refs):
    normed, slot_rows = refs[:2]
    out_refs = refs[3 : 3 + len(which)]
    fill(out_refs, which, normed[...], slot_rows, refs[3 + len(which)])


def dispatch(normed, slot_rows, which, cap, earlier):
    rows, width = normed.shape
    return pl.pallas_call(
        functools.partial(dispatch_kernel, tuple(which)),
        out_shape=[jax.ShapeDtypeStruct((cap, width), BF16)] * len(which),
        in_specs=vmem(2) + [pl.BlockSpec(memory_space=pl.ANY)],
        out_specs=vmem(len(which)),
        scratch_shapes=[pltpu.VMEM((len(which) * cap, rows), BF16)],
        compiler_params=params(),
        cost_estimate=pl.CostEstimate(
            flops=2 * len(which) * cap * rows * width, bytes_accessed=10**6, transcendentals=0
        ),
        name="dispatch",
    )(normed, slot_rows, earlier)


def merge_kernel(narrow, which, tokens, own, cached, w_o, gain, router, hits, slot_rows, *refs):
    state_ref, gates_ref, normed_ref = refs[:3]
    count = len(narrow) + len(which)
    out_refs = refs[3 : 3 + count]
    attended, placing = refs[3 + count :]
    for s in range(own.shape[0]):
        part = cached[s].astype(F32)
        lse = part[HD : HD + 1] + part[HD + 1 : HD + 2] + part[HD + 2 : HD + 3]
        m = own[s, HD + EXT : HD + EXT + 1, :]
        total = own[s, HD : HD + 1, :]
        top = jnp.maximum(m, lse)
        w_cached, w_own = jnp.exp2(lse - top), jnp.exp2(m - top)
        norm = 1.0 / (w_cached + w_own * total)
        merged = part[0:HD] * (w_cached * norm) + own[s, 0:HD, :] * (w_own * norm)
        attended[s * HD : (s + 1) * HD, :] = merged.astype(BF16)
    rows_attended = attended[...].T
    fill(out_refs[: len(narrow)], narrow, rows_attended, slot_rows, placing)
    state = tokens[...].astype(F32) + dot(rows_attended, w_o[...])
    state_ref[...] = state
    mean_square = jnp.mean(state * state, axis=-1, keepdims=True)
    normed = (state * lax.rsqrt(mean_square + EPSILON) * gain[...]).astype(BF16)
    logits = dot(normed, router[...])
    squashed = jnp.where(hits[...] > 0, jax.nn.sigmoid(logits), 0.0)
    gates_ref[...] = squashed / jnp.sum(squashed, axis=1, keepdims=True)
    normed_ref[...] = normed
    fill(out_refs[len(narrow) :], which, normed, slot_rows, placing)


def merge_dispatch(tokens, own, cached, w_o, gain, router, hits, slot_rows, narrow, which, cap):
    lanes = own.shape[0]
    rows, width = tokens.shape
    return pl.pallas_call(
        functools.partial(merge_kernel, tuple(narrow), tuple(which)),
        out_shape=[
            jax.ShapeDtypeStruct((rows, width), F32),
            jax.ShapeDtypeStruct((rows, lanes), F32),
            jax.ShapeDtypeStruct((rows, width), BF16),
        ]
        + [jax.ShapeDtypeStruct((cap, lanes * HD), BF16)] * len(narrow)
        + [jax.ShapeDtypeStruct((cap, width), BF16)] * len(which),
        in_specs=vmem(8),
        out_specs=vmem(3 + len(narrow) + len(which)),
        scratch_shapes=[
            pltpu.VMEM((lanes * HD, rows), BF16),
            pltpu.VMEM((max(len(narrow), len(which)) * cap, rows), BF16),
        ],
        compiler_params=params(),
        cost_estimate=pl.CostEstimate(
            flops=4 * 10**9, bytes_accessed=10 * 10**6, transcendentals=10**5
        ),
        name="merge_and_dispatch",
    )(tokens, own, cached, w_o, gain, router, hits, slot_rows)


def expert_kernel(count, late, *refs):
    x_refs = refs[:count]
    if late:
        attended_refs = refs[count : count + late]
        w_o, gain = refs[count + late : count + late + 2]
        refs = refs[late + 2 :]
    gate_ref, up_ref, down_ref = refs[count : count + 3]
    out_refs = refs[count + 4 : 2 * count + 4]
    x_all, total = refs[2 * count + 4 :]
    cap = x_refs[0].shape[0]
    step = pl.program_id(0)

    @pl.when(step == 0)
    def _():
        for n in range(count):
            x = x_refs[n][...]
            if n < late:
                x = rms_norm(x.astype(F32) + dot(attended_refs[n][...], w_o[...]), gain[...])
            x_all[n * cap : (n + 1) * cap, :] = x

    x = x_all[...]
    gate = dot(x, gate_ref[0])
    up = dot(x, up_ref[0])
    active = (jax.nn.gelu(gate, approximate=True) * up).astype(BF16)
    part = dot(active, down_ref[0])

    @pl.when(step == 0)
    def _():
        total[...] = part

    @pl.when(step > 0)
    def _():
        total[...] += part

    @pl.when(step == pl.num_programs(0) - 1)
    def _():
        for n in range(count):
            out_refs[n][...] = total[n * cap : (n + 1) * cap, :].astype(BF16)


def expert(chunks, w_in, w_out, earlier, late=()):
    count = len(chunks)
    cap, width = chunks[0].shape
    hidden = w_out.shape[1]
    tile = 256
    steps = hidden // tile
    whole = pl.BlockSpec((cap, width), lambda j: (0, 0))
    return pl.pallas_call(
        functools.partial(expert_kernel, count, max(0, len(late) - 2)),
        grid=(steps,),
        out_shape=[jax.ShapeDtypeStruct((cap, width), BF16)] * count,
        in_specs=[whole] * count
        + [pl.BlockSpec(extra.shape, lambda j: (0, 0)) for extra in late]
        + [
            pl.BlockSpec((1, width, tile), lambda j: (0, 0, j)),
            pl.BlockSpec((1, width, tile), lambda j: (0, 0, j + steps)),
            pl.BlockSpec((1, tile, width), lambda j: (0, j, 0)),
            pl.BlockSpec(memory_space=pl.ANY),
        ],
        out_specs=[whole] * count,
        scratch_shapes=[
            pltpu.VMEM((count * cap, width), BF16),
            pltpu.VMEM((count * cap, width), F32),
        ],
        compiler_params=params(),
        cost_estimate=pl.CostEstimate(
            flops=6 * count * cap * width * hidden,
            bytes_accessed=6 * width * hidden,
            transcendentals=count * cap * hidden,
        ),
        name="expert",
    )(*chunks, *late, w_in, w_in, w_out, earlier)


def combine_kernel(which, *refs):
    count = len(which)
    base, gates, slots = refs[:3]
    parts = refs[3 : 3 + count]
    out = refs[3 + count]
    rows = base.shape[0]
    cap = parts[0].shape[0]
    total = base[...]
    for n in range(count):
        s = which[n]
        lane = lax.broadcasted_iota(jnp.int32, (rows, cap), 1)
        pick = (lane == slots[:, s : s + 1]).astype(F32).astype(BF16)
        total = total + gates[:, s : s + 1] * dot(pick, parts[n][...])
    out[...] = total.astype(out.dtype)


def combine(base, gates, slots, parts, which, last):
    count = len(parts)
    rows, width = base.shape
    return pl.pallas_call(
        functools.partial(combine_kernel, tuple(which)),
        out_shape=jax.ShapeDtypeStruct((rows, width), BF16 if last else F32),
        in_specs=vmem(3 + count),
        out_specs=pl.BlockSpec(memory_space=pltpu.VMEM),
        compiler_params=params(),
        cost_estimate=pl.CostEstimate(
            flops=2 * count * rows * parts[0].shape[0] * width,
            bytes_accessed=6 * 10**6,
            transcendentals=0,
        ),
        name="combine",
    )(base, gates, slots, *parts)


def body(
    tokens,
    gain_attn,
    w_qkv,
    w_attn_out,
    kv_cache,
    page_table,
    cached_lengths,
    gain_moe,
    w_router,
    routes,
    w_in,
    w_out,
):
    lanes, groups = lax.axis_size("tensor"), lax.axis_size("batch")
    me, group = lax.axis_index("tensor"), lax.axis_index("batch")
    rows, width = tokens.shape
    requests = cached_lengths.shape[0]
    span_devs = lanes // requests
    share = width // groups
    info = jnp.stack([me, group]).astype(jnp.int32)

    w_t = w_qkv.T
    q_high = gather_high(w_t[0:HD], lanes, groups)
    q_plane = gather_plane(q_high, lanes, groups)
    q_other = send(q_plane, lanes, lanes, groups)
    normed = rms_norm(tokens, gain_attn)
    q = project_queries(info, normed, q_plane, q_other)
    q_here = lax.all_to_all(q, "tensor", split_axis=0, concat_axis=0, tiled=True)

    near = [normed]
    rest = jnp.concatenate([w_t[HD : 3 * HD], w_attn_out.T], axis=0)
    ready, rest = after(normed, q_plane), after(rest, q)
    for i in range(1, span_devs):
        pairs = [
            (b * lanes + t, b * lanes + (t ^ i))
            for b in range(groups)
            for t in range(lanes)
            if t % span_devs < (t ^ i) % span_devs
        ]
        near.append(lax.ppermute(ready, AXES, pairs))
    rest = gather_high(rest, lanes, groups)
    rest = gather_plane(after(rest, q_here, *near[1:]), lanes, groups)

    names = me ^ jnp.arange(lanes, dtype=jnp.int32)
    hit_rows = (routes[:, 0][None, :] == names[:, None]) | (routes[:, 1][None, :] == names[:, None])
    earlier = jnp.triu(jnp.ones((rows, rows), BF16), 1)
    rank = dot(hit_rows.astype(BF16), earlier).astype(jnp.int32)
    slot_rows = jnp.where(hit_rows, rank, -1)
    slots = slot_rows.T
    hits = hit_rows.astype(jnp.int32).T
    capacity = max(2, (5 * rows * routes.shape[1] + 4 * lanes - 1) // (4 * lanes))
    cap = -(-capacity // 16) * 16
    router = jnp.take(w_router, names, axis=1)

    half = lanes // 2
    near_experts = list(range(half))
    far = [list(range(half, lanes, 2)), list(range(half + 1, lanes, 2))]
    ahead = far[0][: max(1, len(far[0]) // 2)]
    early = dispatch(tokens, slot_rows, ahead, cap, tokens)
    early = lax.optimization_barrier((*early, q_here))[:-1]
    early = [send(part, s, lanes, groups) for s, part in zip(ahead, early)]

    parts = cached_attention(cached_lengths, page_table, q_here, kv_cache)
    rest_other = send(after(rest, parts, *early), lanes, lanes, groups)
    cached = lax.all_to_all(parts, "tensor", split_axis=0, concat_axis=0, tiled=True)
    own, w_o = self_attention(info, q, near, rest, rest_other, parts)

    outcome = merge_dispatch(
        tokens,
        own,
        cached,
        w_o,
        gain_moe.reshape(1, width),
        router,
        hits,
        slot_rows,
        ahead,
        far[0][len(ahead) :] + far[1] + near_experts,
        cap,
    )
    state, gates, normed_moe = outcome[:3]
    late = [send(part, s, lanes, groups) for s, part in zip(ahead, outcome[3:])]
    whole = far[0][len(ahead) :] + far[1] + near_experts
    arrived = dict(zip(whole, outcome[3 + len(ahead) :]))
    arrived.update({s: send(arrived[s], s, lanes, groups) for s in whole if s})
    arrived.update(zip(ahead, early))
    mixed = state
    results = [gates]
    for part in (far[0], near_experts, far[1]):
        more = (*late, w_o, gain_moe.reshape(1, width)) if part is far[0] else ()
        results = expert([arrived[s] for s in part], w_in, w_out, results[0], more)
        returned = [
            results[n] if s == 0 else send(results[n], s, lanes, groups)
            for n, s in enumerate(part)
        ]
        mixed = combine(mixed, gates, slots, returned, part, part is far[1])
    return mixed


def solution(mesh):
    in_specs = (
        P(("batch", "tensor"), None),
        P(),
        P("batch", "tensor"),
        P("batch", "tensor"),
        P("batch", None, "tensor"),
        P("batch", None),
        P("batch"),
        P(),
        P(),
        P(("batch", "tensor"), None),
        P("tensor", None, None),
        P("tensor", None, None),
    )
    out_specs = P(("batch", "tensor"), None)
    return jax.shard_map(body, mesh=mesh, in_specs=in_specs, out_specs=out_specs, check_vma=False)
```

```python
import functools
import math

import jax
import jax.numpy as jnp
from jax import lax
from jax.experimental import pallas as pl
from jax.experimental.pallas import tpu as pltpu
from jax.sharding import PartitionSpec as P

HD = 64
EXT = 16
EPSILON = 1e-06
NEGATIVE = -1e30
F32, BF16 = jnp.float32, jnp.bfloat16
NT = (((1,), (1,)), ((), ()))
VMEM_LIMIT = 52 * 1024 * 1024
AXES = ("batch", "tensor")


def dot(a, b, dims=(((1,), (0,)), ((), ()))):
    return lax.dot_general(a, b, dims, preferred_element_type=F32)


def rms_norm(values, gain):
    values = values.astype(F32)
    mean_square = jnp.mean(values * values, axis=-1, keepdims=True)
    return (values * lax.rsqrt(mean_square + EPSILON) * gain).astype(BF16)


def vmem(count):
    return [pl.BlockSpec(memory_space=pltpu.VMEM)] * count


def smem(count):
    return [pl.BlockSpec(memory_space=pltpu.SMEM)] * count


def params():
    return pltpu.CompilerParams(vmem_limit_bytes=VMEM_LIMIT)


def send(value, mask, lanes, groups):
    total = lanes * groups
    return lax.ppermute(value, AXES, [(i, i ^ mask) for i in range(total)])


def gather_high(piece, lanes, groups):
    low = max(1, lanes // 4)
    return jnp.stack([piece] + [send(piece, s, lanes, groups) for s in range(low, lanes, low)])


def gather_plane(block, lanes, groups):
    low = max(1, lanes // 4)
    rows = []
    for j in range(0, groups, 2):
        masks = [j * lanes + s for s in range(low)]
        rows.append(
            jnp.stack([send(block, m, lanes, groups) if m else block for m in masks], axis=1)
        )
    return jnp.stack(rows).reshape((groups // 2, lanes) + block.shape[1:])


def after(value, *others):
    return lax.optimization_barrier((value,) + others)[0]


def ones_rows(keys):
    return jnp.ones((EXT, keys), BF16)


def softmax_steps(scores, values, old):
    tops = [jnp.maximum(m, jnp.max(s, axis=0, keepdims=True)) for s, (m, acc) in zip(scores, old)]
    return [
        (top, acc * jnp.exp2(m - top) + dot(v, jnp.exp2(s - top).astype(BF16)))
        for s, v, top, (m, acc) in zip(scores, values, tops, old)
    ]


def cached_kernel(requests, span_devs, block_pages, lengths, table, q_ref, kv_ref, out_ref, q_all, m_ref, acc_ref):
    page = kv_ref.shape[1]
    pages = table.shape[1] // requests
    rows = q_ref.shape[2]
    queries = rows * span_devs
    keys = block_pages * page
    tile = min(256, queries)
    tiles = [slice(t, t + tile) for t in range(0, queries, tile)]
    q_all[HD : 2 * HD, :] = jnp.zeros((HD, queries), BF16)

    def one_request(request, carry):
        length = lengths[request]
        for i in range(span_devs):
            q_all[0:HD, i * rows : (i + 1) * rows] = q_ref[request * span_devs + i]
        m_ref[...] = jnp.full((1, queries), NEGATIVE, F32)
        acc_ref[...] = jnp.zeros((HD + EXT, queries), F32)

        def block(j, masked):
            parts = [
                kv_ref[
                    table[0, request * pages + jnp.minimum(j * block_pages + n, pages - 1)]
                ]
                for n in range(block_pages)
            ]
            both = jnp.concatenate(parts, axis=0)
            values = jnp.concatenate([both.T[HD : 2 * HD], ones_rows(keys)], axis=0)
            scores = [dot(both, q_all[:, at]) for at in tiles]
            if masked:
                position = j * keys + lax.broadcasted_iota(jnp.int32, scores[0].shape, 0)
                scores = [jnp.where(position < length, s, NEGATIVE) for s in scores]
            old = [(m_ref[:, at], acc_ref[:, at]) for at in tiles]
            new = softmax_steps(scores, [values] * len(tiles), old)
            for at, (top, acc) in zip(tiles, new):
                m_ref[:, at] = top
                acc_ref[:, at] = acc

        whole = length // keys

        def step(j, c):
            block(j, False)
            return c

        lax.fori_loop(0, whole, step, 0)

        @pl.when(whole * keys < length)
        def _():
            block(whole, True)

        total = acc_ref[HD : HD + 1, :]
        lse = m_ref[...] + jnp.log2(total)
        hi = lse.astype(BF16).astype(F32)
        mid = (lse - hi).astype(BF16).astype(F32)
        lo = lse - hi - mid
        at_row = lax.broadcasted_iota(jnp.int32, (EXT, queries), 0)
        stats = jnp.where(
            at_row == 0, hi, jnp.where(at_row == 1, mid, jnp.where(at_row == 2, lo, 0.0))
        ).astype(BF16)
        values = (acc_ref[0:HD, :] * (1.0 / total)).astype(BF16)
        for i in range(span_devs):
            at = slice(i * rows, (i + 1) * rows)
            out_ref[request * span_devs + i, 0:HD, :] = values[:, at]
            out_ref[request * span_devs + i, HD : HD + EXT, :] = stats[:, at]
        return carry

    lax.fori_loop(0, requests, one_request, 0)


def cached_attention(lengths, table, q, kv_cache):
    lanes, _, rows = q.shape
    requests = lengths.shape[0]
    span_devs = lanes // requests
    queries = rows * span_devs
    return pl.pallas_call(
        functools.partial(cached_kernel, requests, span_devs, 8),
        out_shape=jax.ShapeDtypeStruct((lanes, HD + EXT, rows), BF16),
        in_specs=smem(2) + vmem(2),
        out_specs=pl.BlockSpec(memory_space=pltpu.VMEM),
        scratch_shapes=[
            pltpu.VMEM((2 * HD, queries), BF16),
            pltpu.VMEM((1, queries), F32),
            pltpu.VMEM((HD + EXT, queries), F32),
        ],
        compiler_params=params(),
        cost_estimate=pl.CostEstimate(
            flops=24 * 10**9, bytes_accessed=6 * 10**6, transcendentals=8 * 10**6
        ),
        name="cached_attention",
    )(lengths, table, q, kv_cache)


def query_kernel(scale, info, normed, even, odd, out_ref):
    lanes, _, rows = out_ref.shape
    halves, _, _, share = even.shape
    total = jnp.zeros((lanes * HD, rows), F32)
    for n in range(halves):
        for low, ref in enumerate((even, odd)):
            at = jnp.bitwise_xor(info[1], 2 * n + low) * share
            columns = normed[:, pl.ds(pl.multiple_of(at, share), share)]
            total = total + dot(ref[n].reshape(lanes * HD, share), columns, NT)
    q = (total * scale).astype(BF16)
    for s in range(lanes):
        out_ref[jnp.bitwise_xor(info[0], s)] = q[s * HD : (s + 1) * HD]


def project_queries(info, normed, even, odd):
    lanes = even.shape[1]
    rows = normed.shape[0]
    scale = math.log2(math.e) / math.sqrt(HD)
    return pl.pallas_call(
        functools.partial(query_kernel, scale),
        out_shape=jax.ShapeDtypeStruct((lanes, HD, rows), BF16),
        in_specs=smem(1) + vmem(3),
        out_specs=pl.BlockSpec(memory_space=pltpu.VMEM),
        compiler_params=params(),
        cost_estimate=pl.CostEstimate(flops=10**9, bytes_accessed=2 * 10**6, transcendentals=0),
        name="project_queries",
    )(info, normed, even, odd)


def self_kernel(span_devs, *refs):
    info, q_ref = refs[:2]
    normed_refs = refs[2 : 2 + span_devs]
    even, odd = refs[2 + span_devs : 4 + span_devs]
    out_ref, w_o_ref, w_k, w_v, keys_ref, values_ref = refs[5 + span_devs :]
    lanes, _, rows = q_ref.shape
    halves, _, _, share = even.shape
    groups = 2 * halves
    me, group = info[0], info[1]
    at = me % span_devs

    for n in range(halves):
        for low, ref in enumerate((even, odd)):
            column = pl.ds(
                pl.multiple_of(jnp.bitwise_xor(group, 2 * n + low) * share, share), share
            )
            for h in range(lanes):
                piece = ref[n, jnp.bitwise_xor(me, h)]
                head = slice(h * HD, (h + 1) * HD)
                w_k[head, column] = piece[0:HD]
                w_v[head, column] = piece[HD : 2 * HD]
                w_o_ref[head, column] = piece[2 * HD : 3 * HD]

    def project(normed):
        keys_ref[...] = dot(normed[...], w_k[...], NT).astype(BF16)
        values_ref[...] = dot(w_v[...], normed[...], NT).astype(BF16)

    together = 4
    tile = min(256, rows)

    def run(causal):
        def step(g, carry):
            scores, values, old, places = [], [], [], []
            nothing = jnp.zeros((HD, tile), BF16)
            for p in range(together // 2):
                block = pl.multiple_of((g * together + 2 * p) * HD, 2 * HD)
                keys = keys_ref[:, pl.ds(block, 2 * HD)]
                both_v = values_ref[pl.ds(block, 2 * HD), :]
                for h in range(2):
                    s = g * together + 2 * p + h
                    q = q_ref[s]
                    value = jnp.concatenate([both_v[h * HD : (h + 1) * HD], ones_rows(rows)], axis=0)
                    for t in range(0, rows, tile):
                        here = slice(t, t + tile)
                        seen = t + tile if causal else rows
                        part = [nothing, q[:, here]] if h else [q[:, here], nothing]
                        score = dot(keys[0:seen], jnp.concatenate(part, axis=0))
                        if causal:
                            position = lax.broadcasted_iota(jnp.int32, score.shape, 0)
                            line = t + lax.broadcasted_iota(jnp.int32, score.shape, 1)
                            score = jnp.where(position <= line, score, NEGATIVE)
                            m = jnp.full((1, tile), NEGATIVE, F32)
                            acc = jnp.zeros((HD + EXT, tile), F32)
                        else:
                            m = out_ref[s, HD + EXT : HD + EXT + 1, here]
                            acc = out_ref[s, 0 : HD + EXT, here]
                        scores.append(score)
                        values.append(value[:, 0:seen])
                        old.append((m, acc))
                        places.append((s, here))
            for (s, here), (top, acc) in zip(places, softmax_steps(scores, values, old)):
                out_ref[s, 0 : HD + EXT, here] = acc
                out_ref[s, HD + EXT : HD + EXT + 8, here] = jnp.broadcast_to(top, (8, tile))
            return carry

        lax.fori_loop(0, lanes // together, step, 0)

    project(normed_refs[0])
    run(True)
    for other in range(1, span_devs):

        @pl.when(jnp.bitwise_xor(at, other) < at)
        def _(other=other):
            project(normed_refs[other])
            run(False)


def self_attention(info, q, normed, even, odd, earlier):
    span_devs = len(normed)
    lanes, _, rows = q.shape
    width = normed[0].shape[1]
    anywhere = [pl.BlockSpec(memory_space=pl.ANY)]
    return pl.pallas_call(
        functools.partial(self_kernel, span_devs),
        out_shape=[
            jax.ShapeDtypeStruct((lanes, HD + EXT + 8, rows), F32),
            jax.ShapeDtypeStruct((lanes * HD, width), BF16),
        ],
        in_specs=smem(1) + vmem(3 + span_devs) + anywhere,
        out_specs=vmem(2),
        scratch_shapes=[
            pltpu.VMEM((lanes * HD, width), BF16),
            pltpu.VMEM((lanes * HD, width), BF16),
            pltpu.VMEM((rows, lanes * HD), BF16),
            pltpu.VMEM((lanes * HD, rows), BF16),
        ],
        compiler_params=params(),
        cost_estimate=pl.CostEstimate(
            flops=4 * 10**9, bytes_accessed=5 * 10**6, transcendentals=4 * 10**6
        ),
        name="self_attention",
    )(info, q, *normed, even, odd, earlier)


def fill(out_refs, which, values, slot_rows, placing):
    cap = out_refs[0].shape[0]
    rows = values.shape[0]
    for n, s in enumerate(which):
        at_slot = lax.broadcasted_iota(jnp.int32, (cap, rows), 0)
        placing[n * cap : (n + 1) * cap, :] = (
            (at_slot == slot_rows[s : s + 1, :]).astype(F32).astype(BF16)
        )
    rows_out = dot(placing[0 : len(which) * cap, :], values).astype(BF16)
    for n in range(len(which)):
        out_refs[n][...] = rows_out[n * cap : (n + 1) * cap, :]


def dispatch_kernel(which, *refs):
    normed, slot_rows = refs[:2]
    out_refs = refs[3 : 3 + len(which)]
    fill(out_refs, which, normed[...], slot_rows, refs[3 + len(which)])


def dispatch(normed, slot_rows, which, cap, earlier):
    rows, width = normed.shape
    return pl.pallas_call(
        functools.partial(dispatch_kernel, tuple(which)),
        out_shape=[jax.ShapeDtypeStruct((cap, width), BF16)] * len(which),
        in_specs=vmem(2) + [pl.BlockSpec(memory_space=pl.ANY)],
        out_specs=vmem(len(which)),
        scratch_shapes=[pltpu.VMEM((len(which) * cap, rows), BF16)],
        compiler_params=params(),
        cost_estimate=pl.CostEstimate(
            flops=2 * len(which) * cap * rows * width, bytes_accessed=10**6, transcendentals=0
        ),
        name="dispatch",
    )(normed, slot_rows, earlier)


def merge_kernel(narrow, which, tokens, own, cached, w_o, gain, router, hits, slot_rows, *refs):
    state_ref, gates_ref, normed_ref = refs[:3]
    count = len(narrow) + len(which)
    out_refs = refs[3 : 3 + count]
    attended, placing = refs[3 + count :]
    for s in range(own.shape[0]):
        part = cached[s].astype(F32)
        lse = part[HD : HD + 1] + part[HD + 1 : HD + 2] + part[HD + 2 : HD + 3]
        m = own[s, HD + EXT : HD + EXT + 1, :]
        total = own[s, HD : HD + 1, :]
        top = jnp.maximum(m, lse)
        w_cached, w_own = jnp.exp2(lse - top), jnp.exp2(m - top)
        norm = 1.0 / (w_cached + w_own * total)
        merged = part[0:HD] * (w_cached * norm) + own[s, 0:HD, :] * (w_own * norm)
        attended[s * HD : (s + 1) * HD, :] = merged.astype(BF16)
    rows_attended = attended[...].T
    fill(out_refs[: len(narrow)], narrow, rows_attended, slot_rows, placing)
    state = tokens[...].astype(F32) + dot(rows_attended, w_o[...])
    state_ref[...] = state
    mean_square = jnp.mean(state * state, axis=-1, keepdims=True)
    normed = (state * lax.rsqrt(mean_square + EPSILON) * gain[...]).astype(BF16)
    logits = dot(normed, router[...])
    squashed = jnp.where(hits[...] > 0, jax.nn.sigmoid(logits), 0.0)
    gates_ref[...] = squashed / jnp.sum(squashed, axis=1, keepdims=True)
    normed_ref[...] = normed
    fill(out_refs[len(narrow) :], which, normed, slot_rows, placing)


def merge_dispatch(tokens, own, cached, w_o, gain, router, hits, slot_rows, narrow, which, cap):
    lanes = own.shape[0]
    rows, width = tokens.shape
    return pl.pallas_call(
        functools.partial(merge_kernel, tuple(narrow), tuple(which)),
        out_shape=[
            jax.ShapeDtypeStruct((rows, width), F32),
            jax.ShapeDtypeStruct((rows, lanes), F32),
            jax.ShapeDtypeStruct((rows, width), BF16),
        ]
        + [jax.ShapeDtypeStruct((cap, lanes * HD), BF16)] * len(narrow)
        + [jax.ShapeDtypeStruct((cap, width), BF16)] * len(which),
        in_specs=vmem(8),
        out_specs=vmem(3 + len(narrow) + len(which)),
        scratch_shapes=[
            pltpu.VMEM((lanes * HD, rows), BF16),
            pltpu.VMEM((max(len(narrow), len(which)) * cap, rows), BF16),
        ],
        compiler_params=params(),
        cost_estimate=pl.CostEstimate(
            flops=4 * 10**9, bytes_accessed=10 * 10**6, transcendentals=10**5
        ),
        name="merge_and_dispatch",
    )(tokens, own, cached, w_o, gain, router, hits, slot_rows)


def expert_kernel(count, late, *refs):
    x_refs = refs[:count]
    if late:
        attended_refs = refs[count : count + late]
        w_o, gain = refs[count + late : count + late + 2]
        refs = refs[late + 2 :]
    gate_ref, up_ref, down_ref = refs[count : count + 3]
    out_refs = refs[count + 4 : 2 * count + 4]
    x_all, total = refs[2 * count + 4 :]
    cap = x_refs[0].shape[0]
    step = pl.program_id(0)

    @pl.when(step == 0)
    def _():
        for n in range(count):
            x = x_refs[n][...]
            if n < late:
                x = rms_norm(x.astype(F32) + dot(attended_refs[n][...], w_o[...]), gain[...])
            x_all[n * cap : (n + 1) * cap, :] = x

    x = x_all[...]
    gate = dot(x, gate_ref[0])
    up = dot(x, up_ref[0])
    active = (jax.nn.gelu(gate, approximate=True) * up).astype(BF16)
    part = dot(active, down_ref[0])

    @pl.when(step == 0)
    def _():
        total[...] = part

    @pl.when(step > 0)
    def _():
        total[...] += part

    @pl.when(step == pl.num_programs(0) - 1)
    def _():
        for n in range(count):
            out_refs[n][...] = total[n * cap : (n + 1) * cap, :].astype(BF16)


def expert(chunks, w_in, w_out, earlier, late=()):
    count = len(chunks)
    cap, width = chunks[0].shape
    hidden = w_out.shape[1]
    tile = 256
    steps = hidden // tile
    whole = pl.BlockSpec((cap, width), lambda j: (0, 0))
    return pl.pallas_call(
        functools.partial(expert_kernel, count, max(0, len(late) - 2)),
        grid=(steps,),
        out_shape=[jax.ShapeDtypeStruct((cap, width), BF16)] * count,
        in_specs=[whole] * count
        + [pl.BlockSpec(extra.shape, lambda j: (0, 0)) for extra in late]
        + [
            pl.BlockSpec((1, width, tile), lambda j: (0, 0, j)),
            pl.BlockSpec((1, width, tile), lambda j: (0, 0, j + steps)),
            pl.BlockSpec((1, tile, width), lambda j: (0, j, 0)),
            pl.BlockSpec(memory_space=pl.ANY),
        ],
        out_specs=[whole] * count,
        scratch_shapes=[
            pltpu.VMEM((count * cap, width), BF16),
            pltpu.VMEM((count * cap, width), F32),
        ],
        compiler_params=params(),
        cost_estimate=pl.CostEstimate(
            flops=6 * count * cap * width * hidden,
            bytes_accessed=6 * width * hidden,
            transcendentals=count * cap * hidden,
        ),
        name="expert",
    )(*chunks, *late, w_in, w_in, w_out, earlier)


def combine_kernel(which, *refs):
    count = len(which)
    base, gates, slots = refs[:3]
    parts = refs[3 : 3 + count]
    out = refs[3 + count]
    rows = base.shape[0]
    cap = parts[0].shape[0]
    total = base[...]
    for n in range(count):
        s = which[n]
        lane = lax.broadcasted_iota(jnp.int32, (rows, cap), 1)
        pick = (lane == slots[:, s : s + 1]).astype(F32).astype(BF16)
        total = total + gates[:, s : s + 1] * dot(pick, parts[n][...])
    out[...] = total.astype(out.dtype)


def combine(base, gates, slots, parts, which, last):
    count = len(parts)
    rows, width = base.shape
    return pl.pallas_call(
        functools.partial(combine_kernel, tuple(which)),
        out_shape=jax.ShapeDtypeStruct((rows, width), BF16 if last else F32),
        in_specs=vmem(3 + count),
        out_specs=pl.BlockSpec(memory_space=pltpu.VMEM),
        compiler_params=params(),
        cost_estimate=pl.CostEstimate(
            flops=2 * count * rows * parts[0].shape[0] * width,
            bytes_accessed=6 * 10**6,
            transcendentals=0,
        ),
        name="combine",
    )(base, gates, slots, *parts)


def body(
    tokens,
    gain_attn,
    w_qkv,
    w_attn_out,
    kv_cache,
    page_table,
    cached_lengths,
    gain_moe,
    w_router,
    routes,
    w_in,
    w_out,
):
    lanes, groups = lax.axis_size("tensor"), lax.axis_size("batch")
    me, group = lax.axis_index("tensor"), lax.axis_index("batch")
    rows, width = tokens.shape
    requests = cached_lengths.shape[0]
    span_devs = lanes // requests
    share = width // groups
    info = jnp.stack([me, group]).astype(jnp.int32)

    w_t = w_qkv.T
    q_high = gather_high(w_t[0:HD], lanes, groups)
    q_plane = gather_plane(q_high, lanes, groups)
    q_other = send(q_plane, lanes, lanes, groups)
    normed = rms_norm(tokens, gain_attn)
    q = project_queries(info, normed, q_plane, q_other)
    q_here = lax.all_to_all(q, "tensor", split_axis=0, concat_axis=0, tiled=True)

    near = [normed]
    rest = jnp.concatenate([w_t[HD : 3 * HD], w_attn_out.T], axis=0)
    ready, rest = after(normed, q_plane), after(rest, q)
    for i in range(1, span_devs):
        pairs = [
            (b * lanes + t, b * lanes + (t ^ i))
            for b in range(groups)
            for t in range(lanes)
            if t % span_devs < (t ^ i) % span_devs
        ]
        near.append(lax.ppermute(ready, AXES, pairs))
    rest = gather_high(rest, lanes, groups)
    rest = gather_plane(after(rest, q_here, *near[1:]), lanes, groups)

    names = me ^ jnp.arange(lanes, dtype=jnp.int32)
    hit_rows = (routes[:, 0][None, :] == names[:, None]) | (routes[:, 1][None, :] == names[:, None])
    earlier = jnp.triu(jnp.ones((rows, rows), BF16), 1)
    rank = dot(hit_rows.astype(BF16), earlier).astype(jnp.int32)
    slot_rows = jnp.where(hit_rows, rank, -1)
    slots = slot_rows.T
    hits = hit_rows.astype(jnp.int32).T
    capacity = max(2, (5 * rows * routes.shape[1] + 4 * lanes - 1) // (4 * lanes))
    cap = -(-capacity // 16) * 16
    router = jnp.take(w_router, names, axis=1)

    half = lanes // 2
    near_experts = list(range(half))
    far = [list(range(half, lanes, 2)), list(range(half + 1, lanes, 2))]
    ahead = far[0][: max(1, len(far[0]) // 2)]
    early = dispatch(tokens, slot_rows, ahead, cap, tokens)
    early = lax.optimization_barrier((*early, q_here))[:-1]
    early = [send(part, s, lanes, groups) for s, part in zip(ahead, early)]

    parts = cached_attention(cached_lengths, page_table, q_here, kv_cache)
    rest_other = send(after(rest, parts, *early), lanes, lanes, groups)
    cached = lax.all_to_all(parts, "tensor", split_axis=0, concat_axis=0, tiled=True)
    own, w_o = self_attention(info, q, near, rest, rest_other, parts)

    outcome = merge_dispatch(
        tokens,
        own,
        cached,
        w_o,
        gain_moe.reshape(1, width),
        router,
        hits,
        slot_rows,
        ahead,
        far[0][len(ahead) :] + far[1] + near_experts,
        cap,
    )
    state, gates, normed_moe = outcome[:3]
    late = [send(part, s, lanes, groups) for s, part in zip(ahead, outcome[3:])]
    whole = far[0][len(ahead) :] + far[1] + near_experts
    arrived = dict(zip(whole, outcome[3 + len(ahead) :]))
    arrived.update({s: send(arrived[s], s, lanes, groups) for s in whole if s})
    arrived.update(zip(ahead, early))
    mixed = state
    results = [gates]
    for part in (far[0], near_experts, far[1]):
        more = (*late, w_o, gain_moe.reshape(1, width)) if part is far[0] else ()
        results = expert([arrived[s] for s in part], w_in, w_out, results[0], more)
        returned = [
            results[n] if s == 0 else send(results[n], s, lanes, groups)
            for n, s in enumerate(part)
        ]
        final = part[-1:] if part is far[1] else []
        first = part[: len(part) - len(final)]
        mixed = combine(mixed, gates, slots, returned[: len(first)], first, False)
        if final:
            mixed = combine(mixed, gates, slots, returned[len(first) :], final, True)
    return mixed


def solution(mesh):
    in_specs = (
        P(("batch", "tensor"), None),
        P(),
        P("batch", "tensor"),
        P("batch", "tensor"),
        P("batch", None, "tensor"),
        P("batch", None),
        P("batch"),
        P(),
        P(),
        P(("batch", "tensor"), None),
        P("tensor", None, None),
        P("tensor", None, None),
    )
    out_specs = P(("batch", "tensor"), None)
    return jax.shard_map(body, mesh=mesh, in_specs=in_specs, out_specs=out_specs, check_vma=False)
```
